32 devices in a mesh: chan: 8 (over y, x, core), seg: 4 (over z).
Axes of the slice: x: 2, y: 2, z: 4, core: 2. Of those that a mesh axis runs over, the one named last changes fastest.
Arguments:
- traces: bfloat16 [16, 1024, 1792], P('seg', 'chan'), may hold values from -6 to 6
- live_first: int32 [8], P('chan'), may hold values from 0 to 32
- live_end: int32 [8], P('chan'), may hold values from 96 to 128
- tile_owner: int32 [8, 12], replicated, may hold values from 0 to 7, as said below
Outputs:
- cross_stacks: bfloat16 [8, 24, 2, 128, 4096], P('chan', None, None, 'seg')
The draws below stay inside these ranges and needn't reach their ends.
Inputs may be any that keep to these rules, and one draw needn't show every extreme that they name: The 12 tiles of one row block r (tile_owner[r, :]) go to 4 different owners, 3 to each, in an order drawn from the seed. No owner takes more than 24 tiles in all, and one owner takes exactly 24.
All inputs are finite; a program needn't handle non-finite values.
Results may differ from the reference program's by a relative error of at most 0.0068.
Values may be sent and summed in bfloat16 or wider, within the bound.
A program may use at most 128 MiB of HBM per device.

```python
import math
import jax
import jax.numpy as jnp
from jax import lax

SAMPLES = 1792
BINS = 128
F_LOW = 20
SMOOTH = 64
BLK = 128
TILES = 3
ROW_PARTS = 4
QROWS = 32
ITEMS = 12
S_ALL = 16
NB = 8
CHANNELS = 1024
LINK_MOST = 3
RECV_MOST = 24
N_CHAN = 8


def draw_tile_owner(key, part):
    picks = ITEMS // LINK_MOST
    capacity = 2 * ITEMS
    key_bias, key_heavy, key_noise, key_order = jax.random.split(jax.random.fold_in(key, 7), 4)
    owner_bias = jax.random.randint(key_bias, (N_CHAN,), 0, 8)
    heavy_owner = jax.random.randint(key_heavy, (), 0, N_CHAN)
    owner_ids = jnp.arange(N_CHAN, dtype=jnp.int32)
    owner_bias = jnp.where(owner_ids == heavy_owner, 512, owner_bias)
    noise_draw = jax.random.randint(key_noise, (N_CHAN, N_CHAN), 0, 1024)

    def assign(source, carry):
        loads, chosen_all = carry
        scores = (owner_bias * 1024 + noise_draw[source]) * N_CHAN + owner_ids
        room = loads + LINK_MOST <= capacity
        scores = jnp.where(room, scores, -1 - owner_ids)
        chosen = lax.top_k(scores, picks)[1].astype(jnp.int32)
        loads = loads.at[chosen].add(LINK_MOST)
        chosen_all = chosen_all.at[source].set(chosen)
        return (loads, chosen_all)
    start = (jnp.zeros((N_CHAN,), jnp.int32), jnp.zeros((N_CHAN, picks), jnp.int32))
    chosen_all = lax.fori_loop(0, N_CHAN, assign, start)[1]
    orders = jax.vmap(lambda sub_key: jax.random.permutation(sub_key, ITEMS))(jax.random.split(key_order, N_CHAN))
    owners = jnp.take_along_axis(chosen_all, (orders // LINK_MOST).astype(jnp.int32), axis=1)
    return owners.astype(jnp.int32)


def plant(array, own_key, low, largest):
    index_at = [jax.random.randint(jax.random.fold_in(own_key, axis), (), 0, length) for axis, length in enumerate(array.shape)]
    longest = array.shape.index(max(array.shape))
    neighbour = index_at[:longest] + [(index_at[longest] + 1) % array.shape[longest]] + index_at[longest + 1:]
    return array.at[tuple(index_at)].set(low).at[tuple(neighbour)].set(largest)


def block_levels(key, shape, shards, least, top_value):
    def one(axis_at, blocks):
        draws = jax.random.uniform(jax.random.fold_in(jax.random.fold_in(key, 6), axis_at), (blocks,), jnp.float32, least / len(shards), top_value / len(shards))
        return jnp.repeat(jnp.exp(draws), shape[axis_at] // blocks).reshape((-1,) + (1,) * (len(shape) - axis_at - 1))

    gain = one(*shards[0])
    for cut in shards[1:]:
        gain = gain * one(*cut)
    return gain


def bell_draw(own_key, dims, width, limit, cuts=(), held_as=jnp.bfloat16):
    values = width * jax.random.normal(own_key, dims, jnp.float32)
    if cuts:
        values = values * block_levels(own_key, dims, cuts, -0.22, 0.18)
    return jnp.clip(values, -limit, limit).astype(held_as)


def setup_inputs(seed: int = 0) -> dict:
    keys = jax.random.split(jax.random.key(seed), 5)
    traces = bell_draw(keys[0], (S_ALL, CHANNELS, SAMPLES), 1.0, 6.0, ((0, 4), (1, 8)))
    live_first = plant(jax.random.randint(keys[1], (NB,), 0, BLK // 4 + 1), jax.random.fold_in(keys[1], 1), 0, (BLK // 4 + 1) - 1).astype(jnp.int32)
    live_end = plant(jax.random.randint(keys[2], (NB,), BLK - BLK // 4, BLK + 1), jax.random.fold_in(keys[2], 1), BLK - BLK // 4, BLK).astype(jnp.int32)
    tile_owner = draw_tile_owner(jax.random.fold_in(keys[4], 71), 0)
    return {"traces": traces, "live_first": live_first, "live_end": live_end, "tile_owner": tile_owner}


EPSILON = 1e-06

def build_table(piece_count):
    bins_here = BINS // piece_count
    sample_idx = jnp.arange(SAMPLES, dtype=jnp.int32)
    column = jnp.arange(2 * BINS, dtype=jnp.int32)
    piece = column // (2 * bins_here)
    part_index = column // bins_here % 2
    within = column % bins_here
    frequency = F_LOW + piece * bins_here + within
    phase = sample_idx[:, None] * frequency[None, :] % SAMPLES
    angle = 2.0 * math.pi / SAMPLES * phase.astype(jnp.float32)
    taper = 0.5 - 0.5 * jnp.cos(2.0 * math.pi / SAMPLES * (sample_idx.astype(jnp.float32) + 0.5))
    wave = jnp.where(part_index[None, :] == 0, jnp.cos(angle), -jnp.sin(angle))
    return (taper[:, None] * wave).astype(jnp.bfloat16)

def window_matrix():
    bin_from = jnp.arange(BINS, dtype=jnp.int32)[:, None]
    bin_to = jnp.arange(BINS, dtype=jnp.int32)[None, :]
    first_bin = jnp.clip(bin_to - SMOOTH // 2, 0, BINS - SMOOTH)
    inside = (bin_from >= first_bin) & (bin_from < first_bin + SMOOTH)
    return jnp.where(inside, 1.0 / SMOOTH, 0.0).astype(jnp.float32)

def reference(traces, live_first, live_end, tile_owner):
    wave_table = build_table(1).astype(jnp.float32)
    window = window_matrix()
    channel = jnp.arange(CHANNELS, dtype=jnp.int32)
    block_of = channel // BLK
    channel_offset = channel % BLK
    live_mask = ((channel_offset >= live_first[block_of]) & (channel_offset < live_end[block_of])).astype(jnp.float32)

    def one_segment(record):
        spectra = jnp.dot(record.astype(jnp.float32), wave_table, preferred_element_type=jnp.float32)
        real_part = spectra[:, :BINS]
        imag_part = spectra[:, BINS:]
        band_power = real_part * real_part + imag_part * imag_part
        smoothed = jnp.dot(band_power, window, precision=lax.Precision.HIGHEST)
        scaling = 1.0 / jnp.sqrt(smoothed + EPSILON)
        whitened = spectra * jnp.concatenate([scaling, scaling], axis=1) * live_mask[:, None]
        return whitened.astype(jnp.bfloat16)
    whitened = lax.map(one_segment, traces)
    padded = jnp.concatenate([whitened, jnp.zeros((S_ALL, (TILES - 1) * BLK, 2 * BINS), jnp.bfloat16)], axis=1)
    flat_owner = tile_owner.reshape(-1).astype(jnp.int32)
    item_ids = jnp.arange(NB * ITEMS, dtype=jnp.int32)
    earlier = item_ids[None, :] < item_ids[:, None]
    same_owner = flat_owner[:, None] == flat_owner[None, :]
    slot_index = lax.optimization_barrier(jnp.sum((same_owner & earlier).astype(jnp.int32), axis=1)).astype(jnp.int32)
    owner_rows = flat_owner.reshape(NB, ITEMS)
    slot_rows = slot_index.reshape(NB, ITEMS)

    def one_row(carry, row_index):
        start = (row_index * BLK).astype(jnp.int32)
        row_spec = lax.dynamic_slice_in_dim(padded, start, BLK, 1).astype(jnp.float32)
        col_spec = lax.dynamic_slice_in_dim(padded, start, TILES * BLK, 1).astype(jnp.float32)
        row_real, row_imag = (row_spec[:, :, :BINS], row_spec[:, :, BINS:])
        col_real, col_imag = (col_spec[:, :, :BINS], col_spec[:, :, BINS:])
        real_sum = jnp.einsum('sif,sjf->fij', row_real, col_real) + jnp.einsum('sif,sjf->fij', row_imag, col_imag)
        imag_sum = jnp.einsum('sif,sjf->fij', row_imag, col_real) - jnp.einsum('sif,sjf->fij', row_real, col_imag)
        result = jnp.stack([real_sum, imag_sum], axis=0)
        result = result.reshape(2, BINS, ROW_PARTS, QROWS, TILES, BLK)
        result = jnp.transpose(result, (4, 2, 0, 1, 3, 5)).reshape(ITEMS, 2, BINS, QROWS * BLK)
        items_out = (result * (1.0 / S_ALL)).astype(jnp.bfloat16)
        owners = lax.dynamic_index_in_dim(owner_rows, row_index, 0, keepdims=False)
        slots = lax.dynamic_index_in_dim(slot_rows, row_index, 0, keepdims=False)
        carry = carry.at[owners, slots].set(items_out)
        return (carry, None)
    cross_stacks = jnp.zeros((N_CHAN, RECV_MOST, 2, BINS, QROWS * BLK), jnp.bfloat16)
    cross_stacks = lax.scan(one_row, cross_stacks, jnp.arange(NB, dtype=jnp.int32))[0]
    return cross_stacks
```

```python
from functools import partial
import math

import jax
import jax.numpy as jnp
import ml_dtypes
import numpy as np
from jax import lax
from jax.experimental import pallas as pl
from jax.experimental.pallas import tpu as pltpu
from jax.sharding import PartitionSpec as P

SAMPLES = 1792
BINS = 128
F_LOW = 20
SMOOTH = 64
TILES = 3
ROW_PARTS = 4
EPSILON = 1e-06
SUB = 8
MESH = pl.DeviceIdType.MESH


def wave_rows():
    t = np.arange(SAMPLES, dtype=np.int64)
    row = np.arange(2 * BINS)
    bin_of = row // (2 * SUB) * SUB + row % SUB
    part = row // SUB % 2
    phase = (t[None, :] * (F_LOW + bin_of)[:, None]) % SAMPLES
    angle = 2.0 * math.pi / SAMPLES * phase
    taper = 0.5 - 0.5 * np.cos(2.0 * math.pi / SAMPLES * (t + 0.5))
    wave = np.where(part[:, None] == 0, np.cos(angle), -np.sin(angle))
    return (taper[None, :] * wave).astype(np.float32).astype(ml_dtypes.bfloat16)


def window_rows():
    to = np.arange(BINS)[:, None]
    frm = np.arange(BINS)[None, :]
    first = np.clip(to - SMOOTH // 2, 0, BINS - SMOOTH)
    inside = (frm >= first) & (frm < first + SMOOTH)
    return np.where(inside, 1.0 / SMOOTH, 0.0).astype(ml_dtypes.bfloat16)


def nt_dot(a, b):
    return lax.dot_general(a, b, (((1,), (1,)), ((), ())), preferred_element_type=jnp.float32)


def dot(a, b):
    return jnp.dot(a, b, preferred_element_type=jnp.float32)


def whiten_kernel(first_ref, end_ref, traces_ref, wave_ref, window_ref, out_ref):
    segs, width, samples = traces_ref.shape
    pieces, groups = out_ref.shape[0], out_ref.shape[2]
    cols = segs * width
    spec = nt_dot(wave_ref[...], traces_ref[...].reshape(cols, samples))
    spec = spec.reshape(BINS // SUB, 2, SUB, cols)
    power = (spec[:, 0] * spec[:, 0] + spec[:, 1] * spec[:, 1]).reshape(BINS, cols)
    window = window_ref[...]
    high = power.astype(jnp.bfloat16)
    rest = power - high.astype(jnp.float32)
    mid = rest.astype(jnp.bfloat16)
    low = (rest - mid.astype(jnp.float32)).astype(jnp.bfloat16)
    smoothed = dot(window, high) + dot(window, mid) + dot(window, low)
    channel = lax.broadcasted_iota(jnp.int32, (BINS, cols), 1) % width
    live = (channel >= first_ref[0]) & (channel < end_ref[0])
    scaling = jnp.where(live, lax.rsqrt(smoothed + EPSILON), 0.0)
    white = spec * scaling.reshape(BINS // SUB, 1, SUB, cols)
    white = white.reshape(BINS // SUB, 2 * SUB, cols).astype(jnp.bfloat16)
    for s in range(segs):
        part = white[:, :, s * width : (s + 1) * width]
        out_ref[:, s] = part.reshape(pieces, groups, 2 * SUB, width)


def whiten(traces, live_first, live_end, pieces):
    segs, width, samples = traces.shape
    groups = BINS // SUB // pieces
    step = 2
    return pl.pallas_call(
        whiten_kernel,
        grid=(segs // step,),
        in_specs=[
            pl.BlockSpec(memory_space=pltpu.SMEM),
            pl.BlockSpec(memory_space=pltpu.SMEM),
            pl.BlockSpec((step, width, samples), lambda i: (i, 0, 0)),
            pl.BlockSpec((2 * BINS, samples), lambda i: (0, 0)),
            pl.BlockSpec((BINS, BINS), lambda i: (0, 0)),
        ],
        out_specs=pl.BlockSpec((pieces, step, groups, 2 * SUB, width), lambda i: (0, i, 0, 0, 0)),
        out_shape=jax.ShapeDtypeStruct((pieces, segs, groups, 2 * SUB, width), jnp.bfloat16),
        compiler_params=pltpu.CompilerParams(vmem_limit_bytes=40 * 2**20),
        name="whiten",
    )(live_first, live_end, traces, jnp.asarray(wave_rows()), jnp.asarray(window_rows()))


def gather_kernel(dims, mine_ref, out_ref, z_send, z_recv, x_send, x_recv, y_send, y_recv, c_send, c_recv, own_sem):
    X, Y, Z = dims
    segs = mine_ref.shape[1]
    half = segs // 2
    c = lax.axis_index("chan")
    z = lax.axis_index("seg")
    core = c % 2
    x = c // 2 % X
    y = c // 2 // X

    def chan(yy, xx, cc):
        return (yy * X + xx) * 2 + cc

    xs = [lax.rem(x + d, X) for d in range(X)]
    ys = [lax.rem(y + d, Y) for d in range(Y)]
    x_from = [lax.rem(x + X - d, X) for d in range(X)]
    y_from = [lax.rem(y + Y - d, Y) for d in range(Y)]
    zs = [lax.rem(z + d, Z) for d in range(Z)]
    z_from = [lax.rem(z + Z - d, Z) for d in range(Z)]
    sibling = chan(y, x, 1 - core)

    barrier = pltpu.get_barrier_semaphore()
    friends = [(c, zs[d]) for d in range(1, Z)]
    friends += [(chan(y, xs[d], core), z) for d in range(1, X)]
    friends += [(chan(ys[d], x, core), z) for d in range(1, Y)]
    friends += [(sibling, z)]
    for f in friends:
        pl.semaphore_signal(barrier, inc=1, device_id=f, device_id_type=MESH)
    pl.semaphore_wait(barrier, len(friends))

    started = []

    def block(owner, lo, count):
        return out_ref.at[owner, pl.ds(lo, count)]

    own = pltpu.make_async_copy(mine_ref.at[z], block(c, z * segs, segs), own_sem)
    own.start()
    for d in range(Z - 1, 0, -1):
        copy = pltpu.make_async_remote_copy(
            mine_ref.at[zs[d]], block(c, z * segs, segs), z_send.at[d], z_recv.at[d],
            device_id=(c, zs[d]), device_id_type=MESH)
        copy.start()
        started.append(copy)

    def wait_z(d):
        if d == 0:
            own.wait()
        else:
            piece = block(c, z_from[d] * segs, segs)
            pltpu.make_async_remote_copy(
                piece, piece, z_send.at[d], z_recv.at[d], device_id=(c, z_from[d]), device_id_type=MESH
            ).wait_recv()

    if Z <= 4:
        order = sorted(range(Z), key=lambda d: min(d, Z - d))
        chunks = [((d,), z_from[d] * segs, half) for d in order]
    else:
        chunks = [(tuple(range(Z)), 0, Z * half)]

    def send(ref, send_sem, recv_sem, to):
        copy = pltpu.make_async_remote_copy(
            ref, ref, send_sem, recv_sem, device_id=(to, z), device_id_type=MESH)
        copy.start()
        started.append(copy)

    def wait_recv(ref, send_sem, recv_sem):
        pltpu.make_async_remote_copy(
            ref, ref, send_sem, recv_sem, device_id=(sibling, z), device_id_type=MESH
        ).wait_recv()

    def first_hops(k):
        waits, lo, count = chunks[k]
        for d in waits:
            wait_z(d)
        a, b = block(c, lo, count), block(c, lo + count, count)
        for d in range(1, X):
            send(a, x_send.at[k, 0, 0, d], x_recv.at[k, 0, 0, d], chan(y, xs[d], core))
        for d in range(1, Y):
            send(b, y_send.at[k, 1, 0, d], y_recv.at[k, 1, 0, d], chan(ys[d], x, core))
        for d in range(1, Y):
            send(a, y_send.at[k, 0, 0, d], y_recv.at[k, 0, 0, d], chan(ys[d], x, core))
        for d in range(1, X):
            send(b, x_send.at[k, 1, 0, d], x_recv.at[k, 1, 0, d], chan(y, xs[d], core))
        for h, ref in ((0, a), (1, b)):
            send(ref, c_send.at[k, h, 0, 0], c_recv.at[k, h, 0, 0], sibling)

    def second_hops(k):
        _, lo, count = chunks[k]
        for dx in range(1, X):
            a = block(chan(y, x_from[dx], core), lo, count)
            wait_recv(a, x_send.at[k, 0, 0, dx], x_recv.at[k, 0, 0, dx])
            for d in range(1, Y):
                send(a, y_send.at[k, 0, dx, d], y_recv.at[k, 0, dx, d], chan(ys[d], x, core))
            send(a, c_send.at[k, 0, 0, dx], c_recv.at[k, 0, 0, dx], sibling)
        for dy in range(1, Y):
            b = block(chan(y_from[dy], x, core), lo + count, count)
            wait_recv(b, y_send.at[k, 1, 0, dy], y_recv.at[k, 1, 0, dy])
            for d in range(1, X):
                send(b, x_send.at[k, 1, dy, d], x_recv.at[k, 1, dy, d], chan(y, xs[d], core))
            send(b, c_send.at[k, 1, dy, 0], c_recv.at[k, 1, dy, 0], sibling)

    def last_hops(k):
        _, lo, count = chunks[k]
        for dx in range(X):
            for dy in range(1, Y):
                a = block(chan(y_from[dy], x_from[dx], core), lo, count)
                wait_recv(a, y_send.at[k, 0, dx, dy], y_recv.at[k, 0, dx, dy])
                send(a, c_send.at[k, 0, dy, dx], c_recv.at[k, 0, dy, dx], sibling)
        for dy in range(Y):
            for dx in range(1, X):
                b = block(chan(y_from[dy], x_from[dx], core), lo + count, count)
                wait_recv(b, x_send.at[k, 1, dy, dx], x_recv.at[k, 1, dy, dx])
                send(b, c_send.at[k, 1, dy, dx], c_recv.at[k, 1, dy, dx], sibling)

    n = len(chunks)
    for k in range(n + 2):
        if k < n:
            first_hops(k)
        if 0 <= k - 1 < n:
            second_hops(k - 1)
        if 0 <= k - 2 < n:
            last_hops(k - 2)
    for k in range(n):
        _, lo, count = chunks[k]
        for h in range(2):
            for dy in range(Y):
                for dx in range(X):
                    ref = block(chan(y_from[dy], x_from[dx], 1 - core), lo + h * count, count)
                    wait_recv(ref, c_send.at[k, h, dy, dx], c_recv.at[k, h, dy, dx])
    for copy in started:
        copy.wait_send()


def gather(mine, chan_count):
    Z, segs, groups, rows, width = mine.shape
    X = math.isqrt(chan_count // 2)
    Y = chan_count // 2 // X
    n = Z if Z <= 4 else 1
    m = max(X, Y)
    dma = pltpu.SemaphoreType.DMA
    return pl.pallas_call(
        partial(gather_kernel, (X, Y, Z)),
        in_specs=[pl.BlockSpec(memory_space=pl.ANY)],
        out_specs=pl.BlockSpec(memory_space=pl.ANY),
        out_shape=jax.ShapeDtypeStruct((chan_count, Z * segs, groups, rows, width), mine.dtype),
        scratch_shapes=[
            dma((Z,)), dma((Z,)),
            dma((n, 2, m, m)), dma((n, 2, m, m)),
            dma((n, 2, m, m)), dma((n, 2, m, m)),
            dma((n, 2, Y, X)), dma((n, 2, Y, X)),
            dma(()),
        ],
        compiler_params=pltpu.CompilerParams(collective_id=0, has_side_effects=True),
        name="gather",
    )(mine)


def tile_kernel(items, owner_ref, w_ref, pick_ref, mask_ref, out_ref, table, turned):
    blocks, segs, groups, rows, width = w_ref.shape
    depth = segs * rows
    part_rows = width // ROW_PARTS
    slots = table.shape[0]
    step = pl.program_id(0)

    @pl.when(step == 0)
    def _():
        me = lax.axis_index("chan")

        def clear(k, _):
            table[k] = -1
            return 0

        lax.fori_loop(0, slots, clear, 0)

        def one_row(r, n):
            for e in range(items):
                hit = owner_ref[r, e] == me

                @pl.when(hit)
                def _():
                    table[n] = r * items + e

                n = n + hit.astype(jnp.int32)
            return n

        lax.fori_loop(0, blocks, one_row, 0)

        def turn(b, _):
            for g in range(groups):
                w = w_ref[b, :, g].astype(jnp.float32).reshape(segs, 2, SUB, width)
                t = jnp.concatenate([-w[:, 1], w[:, 0]], axis=1)
                turned[b, :, g] = t.astype(jnp.bfloat16)
            return 0

        lax.fori_loop(0, blocks, turn, 0)

    code = table[step]
    r = lax.max(code, 0) // items
    e = lax.max(code, 0) % items
    t = e // ROW_PARTS
    u = e % ROW_PARTS
    real = (code >= 0) & (r + t < blocks)

    @pl.when(jnp.logical_not(real))
    def _():
        out_ref[...] = jnp.zeros_like(out_ref)

    @pl.when(real)
    def _():
        pick = pick_ref[u]
        mask = mask_ref[...]
        together = 2 if groups % 2 == 0 else 1
        for first in range(0, groups, together):
            results = []
            for g in range(first, first + together):
                w = w_ref[r, :, g].reshape(depth, width)
                spread = nt_dot(pick, w).reshape(part_rows, SUB, depth)
                left = (spread * mask[None]).reshape(part_rows * SUB, depth).astype(jnp.bfloat16)
                right = jnp.concatenate(
                    [w_ref[r + t, :, g].reshape(depth, width), turned[r + t, :, g].reshape(depth, width)],
                    axis=1,
                )
                results.append(dot(left, right).reshape(part_rows, SUB, 2 * width))
            both = jnp.concatenate(results, axis=1).astype(jnp.bfloat16)
            for i in range(part_rows):
                for a in range(2):
                    out_ref[0, 0, a, first * SUB : (first + together) * SUB, i * width : (i + 1) * width] = both[
                        i, :, a * width : (a + 1) * width
                    ]


def tiles(gathered, tile_owner):
    blocks, segs, groups, rows, width = gathered.shape
    items = tile_owner.shape[1]
    slots = 2 * items
    depth = segs * rows
    part_rows = width // ROW_PARTS
    pick = np.zeros((ROW_PARTS, part_rows * SUB, width), np.float32)
    for u in range(ROW_PARTS):
        for i in range(part_rows):
            pick[u, i * SUB : (i + 1) * SUB, u * part_rows + i] = 1.0
    mask = np.where(np.arange(depth)[None, :] % SUB == np.arange(SUB)[:, None], 1.0 / segs, 0.0)
    return pl.pallas_call(
        partial(tile_kernel, items),
        grid=(slots,),
        in_specs=[
            pl.BlockSpec(memory_space=pltpu.SMEM),
            pl.BlockSpec(gathered.shape, lambda i: (0, 0, 0, 0, 0)),
            pl.BlockSpec(pick.shape, lambda i: (0, 0, 0)),
            pl.BlockSpec(mask.shape, lambda i: (0, 0)),
        ],
        out_specs=pl.BlockSpec((1, 1, 2, groups * SUB, part_rows * width), lambda i: (0, i, 0, 0, 0)),
        out_shape=jax.ShapeDtypeStruct((1, slots, 2, groups * SUB, part_rows * width), jnp.bfloat16),
        scratch_shapes=[
            pltpu.SMEM((slots,), jnp.int32),
            pltpu.VMEM(gathered.shape, jnp.bfloat16),
        ],
        compiler_params=pltpu.CompilerParams(vmem_limit_bytes=56 * 2**20),
        name="tiles",
    )(tile_owner, gathered, jnp.asarray(pick, jnp.bfloat16), jnp.asarray(mask, jnp.float32))


def per_device(traces, live_first, live_end, tile_owner):
    white = whiten(traces, live_first, live_end, lax.axis_size("seg"))
    gathered = gather(white, lax.axis_size("chan"))
    return tiles(gathered, tile_owner)


def solution(mesh):
    placed = (P("seg", "chan", None), P("chan"), P("chan"), P())
    return jax.shard_map(
        per_device,
        mesh=mesh,
        in_specs=placed,
        out_specs=P("chan", None, None, "seg", None),
        check_vma=False,
    )
```

```python
from functools import partial
import math

import jax
import jax.numpy as jnp
import ml_dtypes
import numpy as np
from jax import lax
from jax.experimental import pallas as pl
from jax.experimental.pallas import tpu as pltpu
from jax.sharding import PartitionSpec as P

SAMPLES = 1792
BINS = 128
F_LOW = 20
SMOOTH = 64
TILES = 3
ROW_PARTS = 4
EPSILON = 1e-06
SUB = 8
MESH = pl.DeviceIdType.MESH


def wave_rows():
    t = np.arange(SAMPLES, dtype=np.int64)
    row = np.arange(2 * BINS)
    bin_of = row // (2 * SUB) * SUB + row % SUB
    part = row // SUB % 2
    phase = (t[None, :] * (F_LOW + bin_of)[:, None]) % SAMPLES
    angle = 2.0 * math.pi / SAMPLES * phase
    taper = 0.5 - 0.5 * np.cos(2.0 * math.pi / SAMPLES * (t + 0.5))
    wave = np.where(part[:, None] == 0, np.cos(angle), -np.sin(angle))
    return (taper[None, :] * wave).astype(np.float32).astype(ml_dtypes.bfloat16)


def window_rows():
    to = np.arange(BINS)[:, None]
    frm = np.arange(BINS)[None, :]
    first = np.clip(to - SMOOTH // 2, 0, BINS - SMOOTH)
    inside = (frm >= first) & (frm < first + SMOOTH)
    return np.where(inside, 1.0 / SMOOTH, 0.0).astype(ml_dtypes.bfloat16)


def nt_dot(a, b):
    return lax.dot_general(a, b, (((1,), (1,)), ((), ())), preferred_element_type=jnp.float32)


def dot(a, b):
    return jnp.dot(a, b, preferred_element_type=jnp.float32)


def whiten_kernel(first_ref, end_ref, traces_ref, wave_ref, window_ref, out_ref):
    segs, width, samples = traces_ref.shape
    pieces, groups = out_ref.shape[0], out_ref.shape[2]
    cols = segs * width
    spec = nt_dot(wave_ref[...], traces_ref[...].reshape(cols, samples))
    spec = spec.reshape(BINS // SUB, 2, SUB, cols)
    power = (spec[:, 0] * spec[:, 0] + spec[:, 1] * spec[:, 1]).reshape(BINS, cols)
    window = window_ref[...]
    high = power.astype(jnp.bfloat16)
    rest = power - high.astype(jnp.float32)
    mid = rest.astype(jnp.bfloat16)
    low = (rest - mid.astype(jnp.float32)).astype(jnp.bfloat16)
    smoothed = dot(window, high) + dot(window, mid) + dot(window, low)
    channel = lax.broadcasted_iota(jnp.int32, (BINS, cols), 1) % width
    live = (channel >= first_ref[0]) & (channel < end_ref[0])
    scaling = jnp.where(live, lax.rsqrt(smoothed + EPSILON), 0.0)
    white = spec * scaling.reshape(BINS // SUB, 1, SUB, cols)
    white = white.reshape(BINS // SUB, 2 * SUB, cols).astype(jnp.bfloat16)
    for s in range(segs):
        part = white[:, :, s * width : (s + 1) * width]
        out_ref[:, s] = part.reshape(pieces, groups, 2 * SUB, width)


def whiten(traces, live_first, live_end, pieces):
    segs, width, samples = traces.shape
    groups = BINS // SUB // pieces
    step = 2
    return pl.pallas_call(
        whiten_kernel,
        grid=(segs // step,),
        in_specs=[
            pl.BlockSpec(memory_space=pltpu.SMEM),
            pl.BlockSpec(memory_space=pltpu.SMEM),
            pl.BlockSpec((step, width, samples), lambda i: (i, 0, 0)),
            pl.BlockSpec((2 * BINS, samples), lambda i: (0, 0)),
            pl.BlockSpec((BINS, BINS), lambda i: (0, 0)),
        ],
        out_specs=pl.BlockSpec((pieces, step, groups, 2 * SUB, width), lambda i: (0, i, 0, 0, 0)),
        out_shape=jax.ShapeDtypeStruct((pieces, segs, groups, 2 * SUB, width), jnp.bfloat16),
        compiler_params=pltpu.CompilerParams(vmem_limit_bytes=40 * 2**20),
        name="whiten",
    )(live_first, live_end, traces, jnp.asarray(wave_rows()), jnp.asarray(window_rows()))


def gather_kernel(dims, mine_ref, out_ref, z_send, z_recv, x_send, x_recv, y_send, y_recv, c_send, c_recv, own_sem):
    X, Y, Z = dims
    segs = mine_ref.shape[1]
    half = segs // 2
    c = lax.axis_index("chan")
    z = lax.axis_index("seg")
    core = c % 2
    x = c // 2 % X
    y = c // 2 // X

    def chan(yy, xx, cc):
        return (yy * X + xx) * 2 + cc

    xs = [lax.rem(x + d, X) for d in range(X)]
    ys = [lax.rem(y + d, Y) for d in range(Y)]
    x_from = [lax.rem(x + X - d, X) for d in range(X)]
    y_from = [lax.rem(y + Y - d, Y) for d in range(Y)]
    zs = [lax.rem(z + d, Z) for d in range(Z)]
    z_from = [lax.rem(z + Z - d, Z) for d in range(Z)]
    sibling = chan(y, x, 1 - core)

    barrier = pltpu.get_barrier_semaphore()
    friends = [(c, zs[d]) for d in range(1, Z)]
    friends += [(chan(y, xs[d], core), z) for d in range(1, X)]
    friends += [(chan(ys[d], x, core), z) for d in range(1, Y)]
    friends += [(sibling, z)]
    for f in friends:
        pl.semaphore_signal(barrier, inc=1, device_id=f, device_id_type=MESH)
    pl.semaphore_wait(barrier, len(friends))

    started = []

    def block(owner, lo, count):
        return out_ref.at[owner, pl.ds(lo, count)]

    own = pltpu.make_async_copy(mine_ref.at[z], block(c, z * segs, segs), own_sem)
    own.start()
    for d in range(1, Z):
        copy = pltpu.make_async_remote_copy(
            mine_ref.at[zs[d]], block(c, z * segs, segs), z_send.at[d], z_recv.at[d],
            device_id=(c, zs[d]), device_id_type=MESH)
        copy.start()
        started.append(copy)

    def wait_z(d):
        if d == 0:
            own.wait()
        else:
            piece = block(c, z_from[d] * segs, segs)
            pltpu.make_async_remote_copy(
                piece, piece, z_send.at[d], z_recv.at[d], device_id=(c, z_from[d]), device_id_type=MESH
            ).wait_recv()

    if Z <= 4:
        order = sorted(range(Z), key=lambda d: min(d, Z - d))
        chunks = [((d,), z_from[d] * segs, half) for d in order]
    else:
        chunks = [(tuple(range(Z)), 0, Z * half)]

    def send(ref, send_sem, recv_sem, to):
        copy = pltpu.make_async_remote_copy(
            ref, ref, send_sem, recv_sem, device_id=(to, z), device_id_type=MESH)
        copy.start()
        started.append(copy)

    def wait_recv(ref, send_sem, recv_sem):
        pltpu.make_async_remote_copy(
            ref, ref, send_sem, recv_sem, device_id=(sibling, z), device_id_type=MESH
        ).wait_recv()

    def first_hops(k):
        waits, lo, count = chunks[k]
        for d in waits:
            wait_z(d)
        a, b = block(c, lo, count), block(c, lo + count, count)
        for d in range(1, X):
            send(a, x_send.at[k, 0, 0, d], x_recv.at[k, 0, 0, d], chan(y, xs[d], core))
        for d in range(1, Y):
            send(b, y_send.at[k, 1, 0, d], y_recv.at[k, 1, 0, d], chan(ys[d], x, core))
        for d in range(1, Y):
            send(a, y_send.at[k, 0, 0, d], y_recv.at[k, 0, 0, d], chan(ys[d], x, core))
        for d in range(1, X):
            send(b, x_send.at[k, 1, 0, d], x_recv.at[k, 1, 0, d], chan(y, xs[d], core))
        for h, ref in ((0, a), (1, b)):
            send(ref, c_send.at[k, h, 0, 0], c_recv.at[k, h, 0, 0], sibling)

    def second_hops(k):
        _, lo, count = chunks[k]
        for dx in range(1, X):
            a = block(chan(y, x_from[dx], core), lo, count)
            wait_recv(a, x_send.at[k, 0, 0, dx], x_recv.at[k, 0, 0, dx])
            for d in range(1, Y):
                send(a, y_send.at[k, 0, dx, d], y_recv.at[k, 0, dx, d], chan(ys[d], x, core))
            send(a, c_send.at[k, 0, 0, dx], c_recv.at[k, 0, 0, dx], sibling)
        for dy in range(1, Y):
            b = block(chan(y_from[dy], x, core), lo + count, count)
            wait_recv(b, y_send.at[k, 1, 0, dy], y_recv.at[k, 1, 0, dy])
            for d in range(1, X):
                send(b, x_send.at[k, 1, dy, d], x_recv.at[k, 1, dy, d], chan(y, xs[d], core))
            send(b, c_send.at[k, 1, dy, 0], c_recv.at[k, 1, dy, 0], sibling)

    def last_hops(k):
        _, lo, count = chunks[k]
        for dx in range(X):
            for dy in range(1, Y):
                a = block(chan(y_from[dy], x_from[dx], core), lo, count)
                wait_recv(a, y_send.at[k, 0, dx, dy], y_recv.at[k, 0, dx, dy])
                send(a, c_send.at[k, 0, dy, dx], c_recv.at[k, 0, dy, dx], sibling)
        for dy in range(Y):
            for dx in range(1, X):
                b = block(chan(y_from[dy], x_from[dx], core), lo + count, count)
                wait_recv(b, x_send.at[k, 1, dy, dx], x_recv.at[k, 1, dy, dx])
                send(b, c_send.at[k, 1, dy, dx], c_recv.at[k, 1, dy, dx], sibling)

    n = len(chunks)
    first_hops(0)
    second_hops(0)
    for k in range(1, n):
        first_hops(k)
    for k in range(1, n):
        second_hops(k)
    for k in range(n):
        last_hops(k)
    for k in range(n):
        _, lo, count = chunks[k]
        for h in range(2):
            for dy in range(Y):
                for dx in range(X):
                    ref = block(chan(y_from[dy], x_from[dx], 1 - core), lo + h * count, count)
                    wait_recv(ref, c_send.at[k, h, dy, dx], c_recv.at[k, h, dy, dx])
    for copy in started:
        copy.wait_send()


def gather(mine, chan_count):
    Z, segs, groups, rows, width = mine.shape
    X = math.isqrt(chan_count // 2)
    Y = chan_count // 2 // X
    n = Z if Z <= 4 else 1
    m = max(X, Y)
    dma = pltpu.SemaphoreType.DMA
    return pl.pallas_call(
        partial(gather_kernel, (X, Y, Z)),
        in_specs=[pl.BlockSpec(memory_space=pltpu.VMEM)],
        out_specs=pl.BlockSpec(memory_space=pltpu.VMEM),
        out_shape=jax.ShapeDtypeStruct((chan_count, Z * segs, groups, rows, width), mine.dtype),
        scratch_shapes=[
            dma((Z,)), dma((Z,)),
            dma((n, 2, m, m)), dma((n, 2, m, m)),
            dma((n, 2, m, m)), dma((n, 2, m, m)),
            dma((n, 2, Y, X)), dma((n, 2, Y, X)),
            dma(()),
        ],
        compiler_params=pltpu.CompilerParams(
            collective_id=0, has_side_effects=True, vmem_limit_bytes=40 * 2**20
        ),
        name="gather",
    )(mine)


def tile_kernel(items, owner_ref, w_ref, out_ref, slot_of, code_of, used, turned, pick, mask, zeros, ring, sems):
    blocks, segs, groups, rows, width = w_ref.shape
    depth = segs * rows
    part_rows = width // ROW_PARTS
    slots = used.shape[0]
    buffers = ring.shape[0]
    me = lax.axis_index("chan")

    def store(source, slot):
        return pltpu.make_async_copy(source, out_ref.at[0, slot], sems.at[slot])

    def clear(k, _):
        used[k] = 0
        return 0

    lax.fori_loop(0, slots, clear, 0)

    def one_row(r, counts):
        n, m = counts
        for e in range(items):
            hit = owner_ref[r, e] == me
            real = hit & (r + e // ROW_PARTS < blocks)

            @pl.when(real)
            def _():
                used[n] = 1
                slot_of[m] = n
                code_of[m] = r * items + e

            n = n + hit.astype(jnp.int32)
            m = m + real.astype(jnp.int32)
        return n, m

    count = lax.fori_loop(0, blocks, one_row, (jnp.int32(0), jnp.int32(0)))[1]

    zeros[...] = jnp.zeros_like(zeros)

    def empty_start(k, _):
        @pl.when(used[k] == 0)
        def _():
            store(zeros, k).start()

        return 0

    lax.fori_loop(0, slots, empty_start, 0)

    def turn(b, _):
        for g in range(groups):
            w = w_ref[b, :, g].astype(jnp.float32).reshape(segs, 2, SUB, width)
            t = jnp.concatenate([-w[:, 1], w[:, 0]], axis=1)
            turned[b, :, g] = t.astype(jnp.bfloat16)
        return 0

    lax.fori_loop(0, blocks, turn, 0)
    row = lax.broadcasted_iota(jnp.int32, (part_rows * SUB, width), 0) // SUB
    col = lax.broadcasted_iota(jnp.int32, (part_rows * SUB, width), 1)
    for u in range(ROW_PARTS):
        pick[u] = jnp.where(row + u * part_rows == col, 1.0, 0.0).astype(jnp.bfloat16)
    bin_row = lax.broadcasted_iota(jnp.int32, (SUB, depth), 0)
    bin_col = lax.broadcasted_iota(jnp.int32, (SUB, depth), 1) % SUB
    mask[...] = jnp.where(bin_row == bin_col, 1.0 / segs, 0.0)

    def one_tile(m, _):
        code = code_of[m]
        r = code // items
        e = code % items
        t = e // ROW_PARTS
        u = e % ROW_PARTS
        buf = m % buffers

        @pl.when(m >= buffers)
        def _():
            store(ring.at[buf], slot_of[lax.max(m - buffers, 0)]).wait()

        together = 2 if groups % 2 == 0 else 1
        for first in range(0, groups, together):
            results = []
            for g in range(first, first + together):
                w = w_ref[r, :, g].reshape(depth, width)
                spread = nt_dot(pick[u], w).reshape(part_rows, SUB, depth)
                left = (spread * mask[...][None]).reshape(part_rows * SUB, depth).astype(jnp.bfloat16)
                right = jnp.concatenate(
                    [w_ref[r + t, :, g].reshape(depth, width), turned[r + t, :, g].reshape(depth, width)],
                    axis=1,
                )
                results.append(dot(left, right).reshape(part_rows, SUB, 2 * width))
            both = jnp.concatenate(results, axis=1).astype(jnp.bfloat16)
            for i in range(part_rows):
                for a in range(2):
                    ring[buf, a, first * SUB : (first + together) * SUB, i * width : (i + 1) * width] = both[
                        i, :, a * width : (a + 1) * width
                    ]
        store(ring.at[buf], slot_of[m]).start()
        return 0

    lax.fori_loop(0, count, one_tile, 0)

    def last(m, _):
        store(ring.at[m % buffers], slot_of[m]).wait()
        return 0

    lax.fori_loop(lax.max(count - buffers, 0), count, last, 0)

    def empty_wait(k, _):
        @pl.when(used[k] == 0)
        def _():
            store(zeros, k).wait()

        return 0

    lax.fori_loop(0, slots, empty_wait, 0)


def tiles(gathered, tile_owner):
    blocks, segs, groups, rows, width = gathered.shape
    items = tile_owner.shape[1]
    slots = 2 * items
    depth = segs * rows
    part_rows = width // ROW_PARTS
    one = (2, groups * SUB, part_rows * width)
    buffers = 6
    return pl.pallas_call(
        partial(tile_kernel, items),
        in_specs=[
            pl.BlockSpec(memory_space=pltpu.SMEM),
            pl.BlockSpec(memory_space=pltpu.VMEM),
        ],
        out_specs=pl.BlockSpec(memory_space=pl.ANY),
        out_shape=jax.ShapeDtypeStruct((1, slots) + one, jnp.bfloat16),
        scratch_shapes=[
            pltpu.SMEM((slots,), jnp.int32),
            pltpu.SMEM((slots,), jnp.int32),
            pltpu.SMEM((slots,), jnp.int32),
            pltpu.VMEM(gathered.shape, jnp.bfloat16),
            pltpu.VMEM((ROW_PARTS, part_rows * SUB, width), jnp.bfloat16),
            pltpu.VMEM((SUB, depth), jnp.float32),
            pltpu.VMEM(one, jnp.bfloat16),
            pltpu.VMEM((buffers,) + one, jnp.bfloat16),
            pltpu.SemaphoreType.DMA((slots,)),
        ],
        compiler_params=pltpu.CompilerParams(vmem_limit_bytes=40 * 2**20),
        name="tiles",
    )(tile_owner, gathered)


def per_device(traces, live_first, live_end, tile_owner):
    white = whiten(traces, live_first, live_end, lax.axis_size("seg"))
    gathered = gather(white, lax.axis_size("chan"))
    return tiles(gathered, tile_owner)


def solution(mesh):
    placed = (P("seg", "chan", None), P("chan"), P("chan"), P())
    return jax.shard_map(
        per_device,
        mesh=mesh,
        in_specs=placed,
        out_specs=P("chan", None, None, "seg", None),
        check_vma=False,
    )
```

```python
from functools import partial
import math

import jax
import jax.numpy as jnp
import ml_dtypes
import numpy as np
from jax import lax
from jax.experimental import pallas as pl
from jax.experimental.pallas import tpu as pltpu
from jax.sharding import PartitionSpec as P

SAMPLES = 1792
BINS = 128
F_LOW = 20
SMOOTH = 64
TILES = 3
ROW_PARTS = 4
EPSILON = 1e-06
SUB = 8
MESH = pl.DeviceIdType.MESH


def wave_rows():
    t = np.arange(SAMPLES, dtype=np.int64)
    row = np.arange(2 * BINS)
    bin_of = row // (2 * SUB) * SUB + row % SUB
    part = row // SUB % 2
    phase = (t[None, :] * (F_LOW + bin_of)[:, None]) % SAMPLES
    angle = 2.0 * math.pi / SAMPLES * phase
    taper = 0.5 - 0.5 * np.cos(2.0 * math.pi / SAMPLES * (t + 0.5))
    wave = np.where(part[:, None] == 0, np.cos(angle), -np.sin(angle))
    return (taper[None, :] * wave).astype(np.float32).astype(ml_dtypes.bfloat16)


def nt_dot(a, b):
    return lax.dot_general(a, b, (((1,), (1,)), ((), ())), preferred_element_type=jnp.float32)


def dot(a, b):
    return jnp.dot(a, b, preferred_element_type=jnp.float32)


def whiten_kernel(first_ref, end_ref, traces_ref, wave_ref, out_ref, traces, wave, wave_sem, traces_sem):
    segs, width, samples = traces.shape
    pieces, groups = out_ref.shape[0], out_ref.shape[2]
    step = 2
    cols = step * width
    half = 2 * BINS // 2
    waves = [
        pltpu.make_async_copy(
            wave_ref.at[pl.ds(i * half, half)], wave.at[pl.ds(i * half, half)], wave_sem.at[i])
        for i in range(2)
    ]
    loads = [pltpu.make_async_copy(traces_ref.at[s], traces.at[s], traces_sem.at[s]) for s in range(segs)]
    for copy in waves + loads:
        copy.start()
    to = lax.broadcasted_iota(jnp.int32, (BINS, BINS), 0)
    frm = lax.broadcasted_iota(jnp.int32, (BINS, BINS), 1)
    lowest = jnp.clip(to - SMOOTH // 2, 0, BINS - SMOOTH)
    inside = (frm >= lowest) & (frm < lowest + SMOOTH)
    window = jnp.where(inside, 1.0 / SMOOTH, 0.0).astype(jnp.bfloat16)
    channel = lax.broadcasted_iota(jnp.int32, (BINS, cols), 1) % width
    live = (channel >= first_ref[0]) & (channel < end_ref[0])
    for copy in waves:
        copy.wait()
    for at in range(0, segs, step):
        for s in range(at, at + step):
            loads[s].wait()
        spec = nt_dot(wave[...], traces[at : at + step].reshape(cols, samples))
        spec = spec.reshape(BINS // SUB, 2, SUB, cols)
        power = (spec[:, 0] * spec[:, 0] + spec[:, 1] * spec[:, 1]).reshape(BINS, cols)
        high = power.astype(jnp.bfloat16)
        rest = power - high.astype(jnp.float32)
        mid = rest.astype(jnp.bfloat16)
        low = (rest - mid.astype(jnp.float32)).astype(jnp.bfloat16)
        smoothed = dot(window, high) + dot(window, mid) + dot(window, low)
        scaling = jnp.where(live, lax.rsqrt(smoothed + EPSILON), 0.0)
        white = spec * scaling.reshape(BINS // SUB, 1, SUB, cols)
        white = white.reshape(BINS // SUB, 2 * SUB, cols).astype(jnp.bfloat16)
        for s in range(step):
            part = white[:, :, s * width : (s + 1) * width]
            out_ref[:, at + s] = part.reshape(pieces, groups, 2 * SUB, width)


def whiten(traces, live_first, live_end, pieces):
    segs, width, samples = traces.shape
    groups = BINS // SUB // pieces
    return pl.pallas_call(
        whiten_kernel,
        in_specs=[
            pl.BlockSpec(memory_space=pltpu.SMEM),
            pl.BlockSpec(memory_space=pltpu.SMEM),
            pl.BlockSpec(memory_space=pltpu.HBM),
            pl.BlockSpec(memory_space=pltpu.HBM),
        ],
        out_specs=pl.BlockSpec(memory_space=pltpu.VMEM),
        out_shape=jax.ShapeDtypeStruct((pieces, segs, groups, 2 * SUB, width), jnp.bfloat16),
        scratch_shapes=[
            pltpu.VMEM(traces.shape, jnp.bfloat16),
            pltpu.VMEM((2 * BINS, samples), jnp.bfloat16),
            pltpu.SemaphoreType.DMA((2,)),
            pltpu.SemaphoreType.DMA((segs,)),
        ],
        compiler_params=pltpu.CompilerParams(vmem_limit_bytes=61 * 2**20),
        name="whiten",
    )(live_first, live_end, traces, jnp.asarray(wave_rows()))


def gather_kernel(dims, mine_ref, out_ref, z_send, z_recv, x_send, x_recv, y_send, y_recv, c_send, c_recv, own_sem):
    X, Y, Z = dims
    segs = mine_ref.shape[1]
    half = segs // 2
    c = lax.axis_index("chan")
    z = lax.axis_index("seg")
    core = c % 2
    x = c // 2 % X
    y = c // 2 // X

    def chan(yy, xx, cc):
        return (yy * X + xx) * 2 + cc

    xs = [lax.rem(x + d, X) for d in range(X)]
    ys = [lax.rem(y + d, Y) for d in range(Y)]
    x_from = [lax.rem(x + X - d, X) for d in range(X)]
    y_from = [lax.rem(y + Y - d, Y) for d in range(Y)]
    if Z == 4:
        near = z - 1 + 2 * ((4 - z) // 4)
        far = 3 - 3 * (z // 2)
        zs = [z, near, 6 - z - near - far, far]
    else:
        zs = [lax.rem(z + d, Z) for d in range(Z)]
    sibling = chan(y, x, 1 - core)

    barrier = pltpu.get_barrier_semaphore()
    friends = [(c, zs[d]) for d in range(1, Z)]
    friends += [(chan(y, xs[d], core), z) for d in range(1, X)]
    friends += [(chan(ys[d], x, core), z) for d in range(1, Y)]
    friends += [(sibling, z)]
    for f in friends:
        pl.semaphore_signal(barrier, inc=1, device_id=f, device_id_type=MESH)
    pl.semaphore_wait(barrier, len(friends))

    started = []

    def block(owner, lo, count):
        return out_ref.at[owner, pl.ds(lo, count)]

    own = pltpu.make_async_copy(mine_ref.at[z], block(c, z * segs, segs), own_sem)
    own.start()
    for d in range(1, Z):
        copy = pltpu.make_async_remote_copy(
            mine_ref.at[zs[d]], block(c, z * segs, segs), z_send.at[d], z_recv.at[z],
            device_id=(c, zs[d]), device_id_type=MESH)
        copy.start()
        started.append(copy)

    def wait_z(d):
        if d == 0:
            own.wait()
        else:
            piece = block(c, zs[d] * segs, segs)
            pltpu.make_async_remote_copy(
                piece, piece, z_send.at[d], z_recv.at[zs[d]], device_id=(c, zs[d]), device_id_type=MESH
            ).wait_recv()

    if Z <= 4:
        chunks = [((d,), zs[d] * segs, half) for d in range(Z)]
    else:
        chunks = [(tuple(range(Z)), 0, Z * half)]

    def send(ref, send_sem, recv_sem, to):
        copy = pltpu.make_async_remote_copy(
            ref, ref, send_sem, recv_sem, device_id=(to, z), device_id_type=MESH)
        copy.start()
        started.append(copy)

    def wait_recv(ref, send_sem, recv_sem):
        pltpu.make_async_remote_copy(
            ref, ref, send_sem, recv_sem, device_id=(sibling, z), device_id_type=MESH
        ).wait_recv()

    def first_hops(k):
        waits, lo, count = chunks[k]
        for d in waits:
            wait_z(d)
        a, b = block(c, lo, count), block(c, lo + count, count)
        for d in range(1, X):
            send(a, x_send.at[k, 0, 0, d], x_recv.at[k, 0, 0, d], chan(y, xs[d], core))
        for d in range(1, Y):
            send(b, y_send.at[k, 1, 0, d], y_recv.at[k, 1, 0, d], chan(ys[d], x, core))
        for d in range(1, Y):
            send(a, y_send.at[k, 0, 0, d], y_recv.at[k, 0, 0, d], chan(ys[d], x, core))
        for d in range(1, X):
            send(b, x_send.at[k, 1, 0, d], x_recv.at[k, 1, 0, d], chan(y, xs[d], core))
        for h, ref in ((0, a), (1, b)):
            send(ref, c_send.at[k, h, 0, 0], c_recv.at[k, h, 0, 0], sibling)

    def second_hops(k):
        _, lo, count = chunks[k]
        for dx in range(1, X):
            a = block(chan(y, x_from[dx], core), lo, count)
            wait_recv(a, x_send.at[k, 0, 0, dx], x_recv.at[k, 0, 0, dx])
            for d in range(1, Y):
                send(a, y_send.at[k, 0, dx, d], y_recv.at[k, 0, dx, d], chan(ys[d], x, core))
            send(a, c_send.at[k, 0, 0, dx], c_recv.at[k, 0, 0, dx], sibling)
        for dy in range(1, Y):
            b = block(chan(y_from[dy], x, core), lo + count, count)
            wait_recv(b, y_send.at[k, 1, 0, dy], y_recv.at[k, 1, 0, dy])
            for d in range(1, X):
                send(b, x_send.at[k, 1, dy, d], x_recv.at[k, 1, dy, d], chan(y, xs[d], core))
            send(b, c_send.at[k, 1, dy, 0], c_recv.at[k, 1, dy, 0], sibling)

    def last_hops(k):
        _, lo, count = chunks[k]
        for dx in range(X):
            for dy in range(1, Y):
                a = block(chan(y_from[dy], x_from[dx], core), lo, count)
                wait_recv(a, y_send.at[k, 0, dx, dy], y_recv.at[k, 0, dx, dy])
                send(a, c_send.at[k, 0, dy, dx], c_recv.at[k, 0, dy, dx], sibling)
        for dy in range(Y):
            for dx in range(1, X):
                b = block(chan(y_from[dy], x_from[dx], core), lo + count, count)
                wait_recv(b, x_send.at[k, 1, dy, dx], x_recv.at[k, 1, dy, dx])
                send(b, c_send.at[k, 1, dy, dx], c_recv.at[k, 1, dy, dx], sibling)

    n = len(chunks)
    first_hops(0)
    second_hops(0)
    for k in range(1, n):
        first_hops(k)
    for k in range(1, n):
        second_hops(k)
    for k in range(n):
        last_hops(k)
    for k in range(n):
        _, lo, count = chunks[k]
        for h in range(2):
            for dy in range(Y):
                for dx in range(X):
                    ref = block(chan(y_from[dy], x_from[dx], 1 - core), lo + h * count, count)
                    wait_recv(ref, c_send.at[k, h, dy, dx], c_recv.at[k, h, dy, dx])
    for copy in started:
        copy.wait_send()


def gather(mine, chan_count):
    Z, segs, groups, rows, width = mine.shape
    X = math.isqrt(chan_count // 2)
    Y = chan_count // 2 // X
    n = Z if Z <= 4 else 1
    m = max(X, Y)
    dma = pltpu.SemaphoreType.DMA
    return pl.pallas_call(
        partial(gather_kernel, (X, Y, Z)),
        in_specs=[pl.BlockSpec(memory_space=pltpu.VMEM)],
        out_specs=pl.BlockSpec(memory_space=pltpu.VMEM),
        out_shape=jax.ShapeDtypeStruct((chan_count, Z * segs, groups, rows, width), mine.dtype),
        scratch_shapes=[
            dma((Z,)), dma((Z,)),
            dma((n, 2, m, m)), dma((n, 2, m, m)),
            dma((n, 2, m, m)), dma((n, 2, m, m)),
            dma((n, 2, Y, X)), dma((n, 2, Y, X)),
            dma(()),
        ],
        compiler_params=pltpu.CompilerParams(
            collective_id=0, has_side_effects=True, vmem_limit_bytes=40 * 2**20
        ),
        name="gather",
    )(mine)


def tile_kernel(items, owner_ref, w_ref, out_ref, slot_of, code_of, used, turned, pick, mask, zeros, ring, sems):
    blocks, segs, groups, rows, width = w_ref.shape
    depth = segs * rows
    part_rows = width // ROW_PARTS
    slots = used.shape[0]
    buffers = ring.shape[0]
    me = lax.axis_index("chan")

    def store(source, slot):
        return pltpu.make_async_copy(source, out_ref.at[0, slot], sems.at[slot])

    def clear(k, _):
        used[k] = 0
        return 0

    lax.fori_loop(0, slots, clear, 0)

    def one_row(r, counts):
        n, m = counts
        for e in range(items):
            hit = owner_ref[r, e] == me
            real = hit & (r + e // ROW_PARTS < blocks)

            @pl.when(real)
            def _():
                used[n] = 1
                slot_of[m] = n
                code_of[m] = r * items + e

            n = n + hit.astype(jnp.int32)
            m = m + real.astype(jnp.int32)
        return n, m

    count = lax.fori_loop(0, blocks, one_row, (jnp.int32(0), jnp.int32(0)))[1]

    zeros[...] = jnp.zeros_like(zeros)

    def empty_start(k, _):
        @pl.when(used[k] == 0)
        def _():
            store(zeros, k).start()

        return 0

    lax.fori_loop(0, slots, empty_start, 0)

    def turn(b, _):
        for g in range(groups):
            w = w_ref[b, :, g].astype(jnp.float32).reshape(segs, 2, SUB, width)
            t = jnp.concatenate([-w[:, 1], w[:, 0]], axis=1)
            turned[b, :, g] = t.astype(jnp.bfloat16)
        return 0

    lax.fori_loop(0, blocks, turn, 0)
    row = lax.broadcasted_iota(jnp.int32, (part_rows * SUB, width), 0) // SUB
    col = lax.broadcasted_iota(jnp.int32, (part_rows * SUB, width), 1)
    for u in range(ROW_PARTS):
        pick[u] = jnp.where(row + u * part_rows == col, 1.0, 0.0).astype(jnp.bfloat16)
    bin_row = lax.broadcasted_iota(jnp.int32, (SUB, depth), 0)
    bin_col = lax.broadcasted_iota(jnp.int32, (SUB, depth), 1) % SUB
    mask[...] = jnp.where(bin_row == bin_col, 1.0 / segs, 0.0)

    def one_tile(m, _):
        code = code_of[m]
        r = code // items
        e = code % items
        t = e // ROW_PARTS
        u = e % ROW_PARTS
        buf = m % buffers

        @pl.when(m >= buffers)
        def _():
            store(ring.at[buf], slot_of[lax.max(m - buffers, 0)]).wait()

        together = 2 if groups % 2 == 0 else 1
        for first in range(0, groups, together):
            results = []
            for g in range(first, first + together):
                w = w_ref[r, :, g].reshape(depth, width)
                spread = nt_dot(pick[u], w).reshape(part_rows, SUB, depth)
                left = (spread * mask[...][None]).reshape(part_rows * SUB, depth).astype(jnp.bfloat16)
                right = jnp.concatenate(
                    [w_ref[r + t, :, g].reshape(depth, width), turned[r + t, :, g].reshape(depth, width)],
                    axis=1,
                )
                results.append(dot(left, right).reshape(part_rows, SUB, 2 * width))
            both = jnp.concatenate(results, axis=1).astype(jnp.bfloat16)
            for i in range(part_rows):
                for a in range(2):
                    ring[buf, a, first * SUB : (first + together) * SUB, i * width : (i + 1) * width] = both[
                        i, :, a * width : (a + 1) * width
                    ]
        store(ring.at[buf], slot_of[m]).start()
        return 0

    lax.fori_loop(0, count, one_tile, 0)

    def last(m, _):
        store(ring.at[m % buffers], slot_of[m]).wait()
        return 0

    lax.fori_loop(lax.max(count - buffers, 0), count, last, 0)

    def empty_wait(k, _):
        @pl.when(used[k] == 0)
        def _():
            store(zeros, k).wait()

        return 0

    lax.fori_loop(0, slots, empty_wait, 0)


def tiles(gathered, tile_owner):
    blocks, segs, groups, rows, width = gathered.shape
    items = tile_owner.shape[1]
    slots = 2 * items
    depth = segs * rows
    part_rows = width // ROW_PARTS
    one = (2, groups * SUB, part_rows * width)
    buffers = 6
    return pl.pallas_call(
        partial(tile_kernel, items),
        in_specs=[
            pl.BlockSpec(memory_space=pltpu.SMEM),
            pl.BlockSpec(memory_space=pltpu.VMEM),
        ],
        out_specs=pl.BlockSpec(memory_space=pl.ANY),
        out_shape=jax.ShapeDtypeStruct((1, slots) + one, jnp.bfloat16),
        scratch_shapes=[
            pltpu.SMEM((slots,), jnp.int32),
            pltpu.SMEM((slots,), jnp.int32),
            pltpu.SMEM((slots,), jnp.int32),
            pltpu.VMEM(gathered.shape, jnp.bfloat16),
            pltpu.VMEM((ROW_PARTS, part_rows * SUB, width), jnp.bfloat16),
            pltpu.VMEM((SUB, depth), jnp.float32),
            pltpu.VMEM(one, jnp.bfloat16),
            pltpu.VMEM((buffers,) + one, jnp.bfloat16),
            pltpu.SemaphoreType.DMA((slots,)),
        ],
        compiler_params=pltpu.CompilerParams(vmem_limit_bytes=40 * 2**20),
        name="tiles",
    )(tile_owner, gathered)


def per_device(traces, live_first, live_end, tile_owner):
    white = whiten(traces, live_first, live_end, lax.axis_size("seg"))
    gathered = gather(white, lax.axis_size("chan"))
    return tiles(gathered, tile_owner)


def solution(mesh):
    placed = (P("seg", "chan", None), P("chan"), P("chan"), P())
    return jax.shard_map(
        per_device,
        mesh=mesh,
        in_specs=placed,
        out_specs=P("chan", None, None, "seg", None),
        check_vma=False,
    )
```

```python
from functools import partial
import math

import jax
import jax.numpy as jnp
import ml_dtypes
import numpy as np
from jax import lax
from jax.experimental import pallas as pl
from jax.experimental.pallas import tpu as pltpu
from jax.sharding import PartitionSpec as P

SAMPLES = 1792
BINS = 128
F_LOW = 20
SMOOTH = 64
TILES = 3
ROW_PARTS = 4
EPSILON = 1e-06
SUB = 8
MESH = pl.DeviceIdType.MESH


def wave_rows():
    t = np.arange(SAMPLES, dtype=np.int64)
    row = np.arange(2 * BINS)
    bin_of = row // (2 * SUB) * SUB + row % SUB
    part = row // SUB % 2
    phase = (t[None, :] * (F_LOW + bin_of)[:, None]) % SAMPLES
    angle = 2.0 * math.pi / SAMPLES * phase
    taper = 0.5 - 0.5 * np.cos(2.0 * math.pi / SAMPLES * (t + 0.5))
    wave = np.where(part[:, None] == 0, np.cos(angle), -np.sin(angle))
    return (taper[None, :] * wave).astype(np.float32).astype(ml_dtypes.bfloat16)


def window_rows():
    to = np.arange(BINS)[:, None]
    frm = np.arange(BINS)[None, :]
    first = np.clip(to - SMOOTH // 2, 0, BINS - SMOOTH)
    inside = (frm >= first) & (frm < first + SMOOTH)
    return np.where(inside, 1.0 / SMOOTH, 0.0).astype(ml_dtypes.bfloat16)


def nt_dot(a, b):
    return lax.dot_general(a, b, (((1,), (1,)), ((), ())), preferred_element_type=jnp.float32)


def dot(a, b):
    return jnp.dot(a, b, preferred_element_type=jnp.float32)


def whiten_kernel(first_ref, end_ref, traces_ref, wave_ref, window_ref, out_ref):
    segs, width, samples = traces_ref.shape
    pieces, groups = out_ref.shape[0], out_ref.shape[2]
    cols = segs * width
    spec = nt_dot(wave_ref[...], traces_ref[...].reshape(cols, samples))
    spec = spec.reshape(BINS // SUB, 2, SUB, cols)
    power = (spec[:, 0] * spec[:, 0] + spec[:, 1] * spec[:, 1]).reshape(BINS, cols)
    window = window_ref[...]
    high = power.astype(jnp.bfloat16)
    rest = power - high.astype(jnp.float32)
    mid = rest.astype(jnp.bfloat16)
    low = (rest - mid.astype(jnp.float32)).astype(jnp.bfloat16)
    smoothed = dot(window, high) + dot(window, mid) + dot(window, low)
    channel = lax.broadcasted_iota(jnp.int32, (BINS, cols), 1) % width
    live = (channel >= first_ref[0]) & (channel < end_ref[0])
    scaling = jnp.where(live, lax.rsqrt(smoothed + EPSILON), 0.0)
    white = spec * scaling.reshape(BINS // SUB, 1, SUB, cols)
    white = white.reshape(BINS // SUB, 2 * SUB, cols).astype(jnp.bfloat16)
    for s in range(segs):
        part = white[:, :, s * width : (s + 1) * width]
        out_ref[:, s] = part.reshape(pieces, groups, 2 * SUB, width)


def whiten(traces, live_first, live_end, pieces):
    segs, width, samples = traces.shape
    groups = BINS // SUB // pieces
    step = 2
    return pl.pallas_call(
        whiten_kernel,
        grid=(segs // step,),
        in_specs=[
            pl.BlockSpec(memory_space=pltpu.SMEM),
            pl.BlockSpec(memory_space=pltpu.SMEM),
            pl.BlockSpec((step, width, samples), lambda i: (i, 0, 0)),
            pl.BlockSpec((2 * BINS, samples), lambda i: (0, 0)),
            pl.BlockSpec((BINS, BINS), lambda i: (0, 0)),
        ],
        out_specs=pl.BlockSpec((pieces, step, groups, 2 * SUB, width), lambda i: (0, i, 0, 0, 0)),
        out_shape=jax.ShapeDtypeStruct((pieces, segs, groups, 2 * SUB, width), jnp.bfloat16),
        compiler_params=pltpu.CompilerParams(vmem_limit_bytes=40 * 2**20),
        name="whiten",
    )(live_first, live_end, traces, jnp.asarray(wave_rows()), jnp.asarray(window_rows()))


def gather_kernel(dims, mine_ref, out_ref, z_send, z_recv, x_send, x_recv, y_send, y_recv, c_send, c_recv, own_sem):
    X, Y, Z = dims
    segs = mine_ref.shape[1]
    half = segs // 2
    c = lax.axis_index("chan")
    z = lax.axis_index("seg")
    core = c % 2
    x = c // 2 % X
    y = c // 2 // X

    def chan(yy, xx, cc):
        return (yy * X + xx) * 2 + cc

    xs = [lax.rem(x + d, X) for d in range(X)]
    ys = [lax.rem(y + d, Y) for d in range(Y)]
    x_from = [lax.rem(x + X - d, X) for d in range(X)]
    y_from = [lax.rem(y + Y - d, Y) for d in range(Y)]
    zs = [lax.rem(z + d, Z) for d in range(Z)]
    z_from = [lax.rem(z + Z - d, Z) for d in range(Z)]
    sibling = chan(y, x, 1 - core)

    barrier = pltpu.get_barrier_semaphore()
    friends = [(c, zs[d]) for d in range(1, Z)]
    friends += [(chan(y, xs[d], core), z) for d in range(1, X)]
    friends += [(chan(ys[d], x, core), z) for d in range(1, Y)]
    friends += [(sibling, z)]
    for f in friends:
        pl.semaphore_signal(barrier, inc=1, device_id=f, device_id_type=MESH)
    pl.semaphore_wait(barrier, len(friends))

    started = []

    def block(owner, lo, count):
        return out_ref.at[owner, pl.ds(lo, count)]

    own = pltpu.make_async_copy(mine_ref.at[z], block(c, z * segs, segs), own_sem)
    own.start()
    for d in range(1, Z):
        copy = pltpu.make_async_remote_copy(
            mine_ref.at[zs[d]], block(c, z * segs, segs), z_send.at[d], z_recv.at[d],
            device_id=(c, zs[d]), device_id_type=MESH)
        copy.start()
        started.append(copy)

    def wait_z(d):
        if d == 0:
            own.wait()
        else:
            piece = block(c, z_from[d] * segs, segs)
            pltpu.make_async_remote_copy(
                piece, piece, z_send.at[d], z_recv.at[d], device_id=(c, z_from[d]), device_id_type=MESH
            ).wait_recv()

    if Z <= 4:
        order = sorted(range(Z), key=lambda d: min(d, Z - d))
        chunks = [((d,), z_from[d] * segs, half) for d in order]
    else:
        chunks = [(tuple(range(Z)), 0, Z * half)]

    def send(ref, send_sem, recv_sem, to):
        copy = pltpu.make_async_remote_copy(
            ref, ref, send_sem, recv_sem, device_id=(to, z), device_id_type=MESH)
        copy.start()
        started.append(copy)

    def wait_recv(ref, send_sem, recv_sem):
        pltpu.make_async_remote_copy(
            ref, ref, send_sem, recv_sem, device_id=(sibling, z), device_id_type=MESH
        ).wait_recv()

    def first_hops(k):
        waits, lo, count = chunks[k]
        for d in waits:
            wait_z(d)
        a, b = block(c, lo, count), block(c, lo + count, count)
        for d in range(1, X):
            send(a, x_send.at[k, 0, 0, d], x_recv.at[k, 0, 0, d], chan(y, xs[d], core))
        for d in range(1, Y):
            send(b, y_send.at[k, 1, 0, d], y_recv.at[k, 1, 0, d], chan(ys[d], x, core))
        for d in range(1, Y):
            send(a, y_send.at[k, 0, 0, d], y_recv.at[k, 0, 0, d], chan(ys[d], x, core))
        for d in range(1, X):
            send(b, x_send.at[k, 1, 0, d], x_recv.at[k, 1, 0, d], chan(y, xs[d], core))
        for h, ref in ((0, a), (1, b)):
            send(ref, c_send.at[k, h, 0, 0], c_recv.at[k, h, 0, 0], sibling)

    def second_hops(k):
        _, lo, count = chunks[k]
        for dx in range(1, X):
            a = block(chan(y, x_from[dx], core), lo, count)
            wait_recv(a, x_send.at[k, 0, 0, dx], x_recv.at[k, 0, 0, dx])
            for d in range(1, Y):
                send(a, y_send.at[k, 0, dx, d], y_recv.at[k, 0, dx, d], chan(ys[d], x, core))
            send(a, c_send.at[k, 0, 0, dx], c_recv.at[k, 0, 0, dx], sibling)
        for dy in range(1, Y):
            b = block(chan(y_from[dy], x, core), lo + count, count)
            wait_recv(b, y_send.at[k, 1, 0, dy], y_recv.at[k, 1, 0, dy])
            for d in range(1, X):
                send(b, x_send.at[k, 1, dy, d], x_recv.at[k, 1, dy, d], chan(y, xs[d], core))
            send(b, c_send.at[k, 1, dy, 0], c_recv.at[k, 1, dy, 0], sibling)

    def last_hops(k):
        _, lo, count = chunks[k]
        for dx in range(X):
            for dy in range(1, Y):
                a = block(chan(y_from[dy], x_from[dx], core), lo, count)
                wait_recv(a, y_send.at[k, 0, dx, dy], y_recv.at[k, 0, dx, dy])
                send(a, c_send.at[k, 0, dy, dx], c_recv.at[k, 0, dy, dx], sibling)
        for dy in range(Y):
            for dx in range(1, X):
                b = block(chan(y_from[dy], x_from[dx], core), lo + count, count)
                wait_recv(b, x_send.at[k, 1, dy, dx], x_recv.at[k, 1, dy, dx])
                send(b, c_send.at[k, 1, dy, dx], c_recv.at[k, 1, dy, dx], sibling)

    n = len(chunks)
    first_hops(0)
    second_hops(0)
    for k in range(1, n):
        first_hops(k)
    for k in range(1, n):
        second_hops(k)
    for k in range(n):
        last_hops(k)
    for k in range(n):
        _, lo, count = chunks[k]
        for h in range(2):
            for dy in range(Y):
                for dx in range(X):
                    ref = block(chan(y_from[dy], x_from[dx], 1 - core), lo + h * count, count)
                    wait_recv(ref, c_send.at[k, h, dy, dx], c_recv.at[k, h, dy, dx])
    for copy in started:
        copy.wait_send()


def gather(mine, chan_count):
    Z, segs, groups, rows, width = mine.shape
    X = math.isqrt(chan_count // 2)
    Y = chan_count // 2 // X
    n = Z if Z <= 4 else 1
    m = max(X, Y)
    dma = pltpu.SemaphoreType.DMA
    return pl.pallas_call(
        partial(gather_kernel, (X, Y, Z)),
        in_specs=[pl.BlockSpec(memory_space=pltpu.VMEM)],
        out_specs=pl.BlockSpec(memory_space=pltpu.VMEM),
        out_shape=jax.ShapeDtypeStruct((chan_count, Z * segs, groups, rows, width), mine.dtype),
        scratch_shapes=[
            dma((Z,)), dma((Z,)),
            dma((n, 2, m, m)), dma((n, 2, m, m)),
            dma((n, 2, m, m)), dma((n, 2, m, m)),
            dma((n, 2, Y, X)), dma((n, 2, Y, X)),
            dma(()),
        ],
        compiler_params=pltpu.CompilerParams(
            collective_id=0, has_side_effects=True, vmem_limit_bytes=40 * 2**20
        ),
        name="gather",
    )(mine)


def tile_kernel(items, owner_ref, w_ref, out_ref, slot_of, code_of, used, turned, pick, mask, zeros, ring, sems, few):
    blocks, segs, groups, rows, width = w_ref.shape
    depth = segs * rows
    part_rows = width // ROW_PARTS
    slots = used.shape[0]
    buffers = ring.shape[0]
    me = lax.axis_index("chan")

    def store(source, slot):
        return pltpu.make_async_copy(source, out_ref.at[0, slot], sems.at[slot])

    def clear(k, _):
        used[k] = 0
        return 0

    lax.fori_loop(0, slots, clear, 0)

    def one_row(r, counts):
        n, m = counts
        for e in range(items):
            hit = owner_ref[r, e] == me
            real = hit & (r + e // ROW_PARTS < blocks)

            @pl.when(real)
            def _():
                used[n] = 1
                slot_of[m] = n
                code_of[m] = r * items + e

            n = n + hit.astype(jnp.int32)
            m = m + real.astype(jnp.int32)
        return n, m

    count = lax.fori_loop(0, blocks, one_row, (jnp.int32(0), jnp.int32(0)))[1]

    zeros[...] = jnp.zeros_like(zeros)

    def empty_start(k, _):
        @pl.when(used[k] == 0)
        def _():
            store(zeros, k).start()

        return 0

    lax.fori_loop(0, slots, empty_start, 0)

    def turn(b, _):
        for g in range(groups):
            w = w_ref[b, :, g].astype(jnp.float32).reshape(segs, 2, SUB, width)
            t = jnp.concatenate([-w[:, 1], w[:, 0]], axis=1)
            turned[b, :, g] = t.astype(jnp.bfloat16)
        return 0

    lax.fori_loop(0, blocks, turn, 0)
    row = lax.broadcasted_iota(jnp.int32, (part_rows * SUB, width), 0) // SUB
    col = lax.broadcasted_iota(jnp.int32, (part_rows * SUB, width), 1)
    few_row = lax.broadcasted_iota(jnp.int32, (part_rows, width), 0)
    for u in range(ROW_PARTS):
        pick[u] = jnp.where(row + u * part_rows == col, 1.0, 0.0).astype(jnp.bfloat16)
        few[u] = jnp.where(few_row + u * part_rows == col[:part_rows], 1.0, 0.0).astype(jnp.bfloat16)
    bin_row = lax.broadcasted_iota(jnp.int32, (SUB, depth), 0)
    bin_col = lax.broadcasted_iota(jnp.int32, (SUB, depth), 1) % SUB
    mask[...] = jnp.where(bin_row == bin_col, 1.0 / segs, 0.0)

    def one_tile(m, _):
        code = code_of[m]
        r = code // items
        e = code % items
        t = e // ROW_PARTS
        u = e % ROW_PARTS
        buf = m % buffers

        @pl.when(m >= buffers)
        def _():
            store(ring.at[buf], slot_of[lax.max(m - buffers, 0)]).wait()

        together = 2 if groups % 2 == 0 else 1
        for first in range(0, groups, together):
            results = []
            for g in range(first, first + together):
                w = w_ref[r, :, g].reshape(depth, width)
                if g % 2 == 0:
                    spread = nt_dot(pick[u], w).reshape(part_rows, SUB, depth)
                else:
                    spread = nt_dot(few[u], w)[:, None, :]
                left = (spread * mask[...][None]).reshape(part_rows * SUB, depth).astype(jnp.bfloat16)
                right = jnp.concatenate(
                    [w_ref[r + t, :, g].reshape(depth, width), turned[r + t, :, g].reshape(depth, width)],
                    axis=1,
                )
                results.append(dot(left, right).reshape(part_rows, SUB, 2 * width))
            both = jnp.concatenate(results, axis=1).astype(jnp.bfloat16)
            for i in range(part_rows):
                for a in range(2):
                    ring[buf, a, first * SUB : (first + together) * SUB, i * width : (i + 1) * width] = both[
                        i, :, a * width : (a + 1) * width
                    ]
        store(ring.at[buf], slot_of[m]).start()
        return 0

    lax.fori_loop(0, count, one_tile, 0)

    def last(m, _):
        store(ring.at[m % buffers], slot_of[m]).wait()
        return 0

    lax.fori_loop(lax.max(count - buffers, 0), count, last, 0)

    def empty_wait(k, _):
        @pl.when(used[k] == 0)
        def _():
            store(zeros, k).wait()

        return 0

    lax.fori_loop(0, slots, empty_wait, 0)


def tiles(gathered, tile_owner):
    blocks, segs, groups, rows, width = gathered.shape
    items = tile_owner.shape[1]
    slots = 2 * items
    depth = segs * rows
    part_rows = width // ROW_PARTS
    one = (2, groups * SUB, part_rows * width)
    buffers = 6
    return pl.pallas_call(
        partial(tile_kernel, items),
        in_specs=[
            pl.BlockSpec(memory_space=pltpu.SMEM),
            pl.BlockSpec(memory_space=pltpu.VMEM),
        ],
        out_specs=pl.BlockSpec(memory_space=pl.ANY),
        out_shape=jax.ShapeDtypeStruct((1, slots) + one, jnp.bfloat16),
        scratch_shapes=[
            pltpu.SMEM((slots,), jnp.int32),
            pltpu.SMEM((slots,), jnp.int32),
            pltpu.SMEM((slots,), jnp.int32),
            pltpu.VMEM(gathered.shape, jnp.bfloat16),
            pltpu.VMEM((ROW_PARTS, part_rows * SUB, width), jnp.bfloat16),
            pltpu.VMEM((SUB, depth), jnp.float32),
            pltpu.VMEM(one, jnp.bfloat16),
            pltpu.VMEM((buffers,) + one, jnp.bfloat16),
            pltpu.SemaphoreType.DMA((slots,)),
            pltpu.VMEM((ROW_PARTS, part_rows, width), jnp.bfloat16),
        ],
        compiler_params=pltpu.CompilerParams(vmem_limit_bytes=40 * 2**20),
        name="tiles",
    )(tile_owner, gathered)


def per_device(traces, live_first, live_end, tile_owner):
    white = whiten(traces, live_first, live_end, lax.axis_size("seg"))
    gathered = gather(white, lax.axis_size("chan"))
    return tiles(gathered, tile_owner)


def solution(mesh):
    placed = (P("seg", "chan", None), P("chan"), P("chan"), P())
    return jax.shard_map(
        per_device,
        mesh=mesh,
        in_specs=placed,
        out_specs=P("chan", None, None, "seg", None),
        check_vma=False,
    )
```

```python
from functools import partial
import math

import jax
import jax.numpy as jnp
import ml_dtypes
import numpy as np
from jax import lax
from jax.experimental import pallas as pl
from jax.experimental.pallas import tpu as pltpu
from jax.sharding import PartitionSpec as P

SAMPLES = 1792
BINS = 128
F_LOW = 20
SMOOTH = 64
TILES = 3
ROW_PARTS = 4
EPSILON = 1e-06
SUB = 8
MESH = pl.DeviceIdType.MESH


def wave_rows():
    t = np.arange(SAMPLES, dtype=np.int64)
    row = np.arange(2 * BINS)
    bin_of = row // (2 * SUB) * SUB + row % SUB
    part = row // SUB % 2
    phase = (t[None, :] * (F_LOW + bin_of)[:, None]) % SAMPLES
    angle = 2.0 * math.pi / SAMPLES * phase
    taper = 0.5 - 0.5 * np.cos(2.0 * math.pi / SAMPLES * (t + 0.5))
    wave = np.where(part[:, None] == 0, np.cos(angle), -np.sin(angle))
    return (taper[None, :] * wave).astype(np.float32).astype(ml_dtypes.bfloat16)


def nt_dot(a, b):
    return lax.dot_general(a, b, (((1,), (1,)), ((), ())), preferred_element_type=jnp.float32)


def dot(a, b):
    return jnp.dot(a, b, preferred_element_type=jnp.float32)


def whiten_kernel(first_ref, end_ref, traces_ref, wave_ref, out_ref):
    segs, width, samples = traces_ref.shape
    pieces, groups = out_ref.shape[0], out_ref.shape[2]
    cols = segs * width
    spec = nt_dot(wave_ref[...], traces_ref[...].reshape(cols, samples))
    spec = spec.reshape(BINS // SUB, 2, SUB, cols)
    power = (spec[:, 0] * spec[:, 0] + spec[:, 1] * spec[:, 1]).reshape(BINS, cols)
    to = lax.broadcasted_iota(jnp.int32, (BINS, BINS), 0)
    frm = lax.broadcasted_iota(jnp.int32, (BINS, BINS), 1)
    lowest = jnp.clip(to - SMOOTH // 2, 0, BINS - SMOOTH)
    inside = (frm >= lowest) & (frm < lowest + SMOOTH)
    window = jnp.where(inside, 1.0 / SMOOTH, 0.0).astype(jnp.bfloat16)
    high = power.astype(jnp.bfloat16)
    rest = power - high.astype(jnp.float32)
    mid = rest.astype(jnp.bfloat16)
    low = (rest - mid.astype(jnp.float32)).astype(jnp.bfloat16)
    smoothed = dot(window, high) + dot(window, mid) + dot(window, low)
    channel = lax.broadcasted_iota(jnp.int32, (BINS, cols), 1) % width
    live = (channel >= first_ref[0]) & (channel < end_ref[0])
    scaling = jnp.where(live, lax.rsqrt(smoothed + EPSILON), 0.0)
    white = spec * scaling.reshape(BINS // SUB, 1, SUB, cols)
    white = white.reshape(BINS // SUB, 2 * SUB, cols).astype(jnp.bfloat16)
    for s in range(segs):
        part = white[:, :, s * width : (s + 1) * width]
        out_ref[:, s] = part.reshape(pieces, groups, 2 * SUB, width)


def whiten(traces, live_first, live_end, pieces):
    segs, width, samples = traces.shape
    groups = BINS // SUB // pieces
    step = 2
    return pl.pallas_call(
        whiten_kernel,
        grid=(segs // step,),
        in_specs=[
            pl.BlockSpec(memory_space=pltpu.SMEM),
            pl.BlockSpec(memory_space=pltpu.SMEM),
            pl.BlockSpec((step, width, samples), lambda i: (i, 0, 0)),
            pl.BlockSpec((2 * BINS, samples), lambda i: (0, 0)),
        ],
        out_specs=pl.BlockSpec((pieces, step, groups, 2 * SUB, width), lambda i: (0, i, 0, 0, 0)),
        out_shape=jax.ShapeDtypeStruct((pieces, segs, groups, 2 * SUB, width), jnp.bfloat16),
        compiler_params=pltpu.CompilerParams(vmem_limit_bytes=40 * 2**20),
        name="whiten",
    )(live_first, live_end, traces, jnp.asarray(wave_rows()))


def gather_kernel(dims, mine_ref, out_ref, z_send, z_recv, x_send, x_recv, y_send, y_recv, c_send, c_recv, own_sem):
    X, Y, Z = dims
    segs = mine_ref.shape[1]
    half = segs // 2
    c = lax.axis_index("chan")
    z = lax.axis_index("seg")
    core = c % 2
    x = c // 2 % X
    y = c // 2 // X

    def chan(yy, xx, cc):
        return (yy * X + xx) * 2 + cc

    xs = [lax.rem(x + d, X) for d in range(X)]
    ys = [lax.rem(y + d, Y) for d in range(Y)]
    x_from = [lax.rem(x + X - d, X) for d in range(X)]
    y_from = [lax.rem(y + Y - d, Y) for d in range(Y)]
    zs = [lax.rem(z + d, Z) for d in range(Z)]
    z_from = [lax.rem(z + Z - d, Z) for d in range(Z)]
    sibling = chan(y, x, 1 - core)

    barrier = pltpu.get_barrier_semaphore()
    friends = [(c, zs[d]) for d in range(1, Z)]
    friends += [(chan(y, xs[d], core), z) for d in range(1, X)]
    friends += [(chan(ys[d], x, core), z) for d in range(1, Y)]
    friends += [(sibling, z)]
    for f in friends:
        pl.semaphore_signal(barrier, inc=1, device_id=f, device_id_type=MESH)
    pl.semaphore_wait(barrier, len(friends))

    started = []

    def block(owner, lo, count):
        return out_ref.at[owner, pl.ds(lo, count)]

    own = pltpu.make_async_copy(mine_ref.at[z], block(c, z * segs, segs), own_sem)
    own.start()
    for d in range(1, Z):
        copy = pltpu.make_async_remote_copy(
            mine_ref.at[zs[d]], block(c, z * segs, segs), z_send.at[d], z_recv.at[d],
            device_id=(c, zs[d]), device_id_type=MESH)
        copy.start()
        started.append(copy)

    def wait_z(d):
        if d == 0:
            own.wait()
        else:
            piece = block(c, z_from[d] * segs, segs)
            pltpu.make_async_remote_copy(
                piece, piece, z_send.at[d], z_recv.at[d], device_id=(c, z_from[d]), device_id_type=MESH
            ).wait_recv()

    if Z <= 4:
        order = sorted(range(Z), key=lambda d: min(d, Z - d))
        chunks = [((d,), z_from[d] * segs, half) for d in order]
    else:
        chunks = [(tuple(range(Z)), 0, Z * half)]

    def send(ref, send_sem, recv_sem, to):
        copy = pltpu.make_async_remote_copy(
            ref, ref, send_sem, recv_sem, device_id=(to, z), device_id_type=MESH)
        copy.start()
        started.append(copy)

    def wait_recv(ref, send_sem, recv_sem):
        pltpu.make_async_remote_copy(
            ref, ref, send_sem, recv_sem, device_id=(sibling, z), device_id_type=MESH
        ).wait_recv()

    def first_hops(k):
        waits, lo, count = chunks[k]
        for d in waits:
            wait_z(d)
        a, b = block(c, lo, count), block(c, lo + count, count)
        for d in range(1, X):
            send(a, x_send.at[k, 0, 0, d], x_recv.at[k, 0, 0, d], chan(y, xs[d], core))
        for d in range(1, Y):
            send(b, y_send.at[k, 1, 0, d], y_recv.at[k, 1, 0, d], chan(ys[d], x, core))
        for d in range(1, Y):
            send(a, y_send.at[k, 0, 0, d], y_recv.at[k, 0, 0, d], chan(ys[d], x, core))
        for d in range(1, X):
            send(b, x_send.at[k, 1, 0, d], x_recv.at[k, 1, 0, d], chan(y, xs[d], core))
        for h, ref in ((0, a), (1, b)):
            send(ref, c_send.at[k, h, 0, 0], c_recv.at[k, h, 0, 0], sibling)

    def second_hops(k):
        _, lo, count = chunks[k]
        for dx in range(1, X):
            a = block(chan(y, x_from[dx], core), lo, count)
            wait_recv(a, x_send.at[k, 0, 0, dx], x_recv.at[k, 0, 0, dx])
            for d in range(1, Y):
                send(a, y_send.at[k, 0, dx, d], y_recv.at[k, 0, dx, d], chan(ys[d], x, core))
            send(a, c_send.at[k, 0, 0, dx], c_recv.at[k, 0, 0, dx], sibling)
        for dy in range(1, Y):
            b = block(chan(y_from[dy], x, core), lo + count, count)
            wait_recv(b, y_send.at[k, 1, 0, dy], y_recv.at[k, 1, 0, dy])
            for d in range(1, X):
                send(b, x_send.at[k, 1, dy, d], x_recv.at[k, 1, dy, d], chan(y, xs[d], core))
            send(b, c_send.at[k, 1, dy, 0], c_recv.at[k, 1, dy, 0], sibling)

    def last_hops(k):
        _, lo, count = chunks[k]
        for dx in range(X):
            for dy in range(1, Y):
                a = block(chan(y_from[dy], x_from[dx], core), lo, count)
                wait_recv(a, y_send.at[k, 0, dx, dy], y_recv.at[k, 0, dx, dy])
                send(a, c_send.at[k, 0, dy, dx], c_recv.at[k, 0, dy, dx], sibling)
        for dy in range(Y):
            for dx in range(1, X):
                b = block(chan(y_from[dy], x_from[dx], core), lo + count, count)
                wait_recv(b, x_send.at[k, 1, dy, dx], x_recv.at[k, 1, dy, dx])
                send(b, c_send.at[k, 1, dy, dx], c_recv.at[k, 1, dy, dx], sibling)

    n = len(chunks)
    first_hops(0)
    second_hops(0)
    for k in range(1, n):
        first_hops(k)
    for k in range(1, n):
        second_hops(k)
    for k in range(n):
        last_hops(k)
    for k in range(n):
        _, lo, count = chunks[k]
        for h in range(2):
            for dy in range(Y):
                for dx in range(X):
                    ref = block(chan(y_from[dy], x_from[dx], 1 - core), lo + h * count, count)
                    wait_recv(ref, c_send.at[k, h, dy, dx], c_recv.at[k, h, dy, dx])
    for copy in started:
        copy.wait_send()


def gather(mine, chan_count):
    Z, segs, groups, rows, width = mine.shape
    X = math.isqrt(chan_count // 2)
    Y = chan_count // 2 // X
    n = Z if Z <= 4 else 1
    m = max(X, Y)
    dma = pltpu.SemaphoreType.DMA
    return pl.pallas_call(
        partial(gather_kernel, (X, Y, Z)),
        in_specs=[pl.BlockSpec(memory_space=pltpu.VMEM)],
        out_specs=pl.BlockSpec(memory_space=pltpu.VMEM),
        out_shape=jax.ShapeDtypeStruct((chan_count, Z * segs, groups, rows, width), mine.dtype),
        scratch_shapes=[
            dma((Z,)), dma((Z,)),
            dma((n, 2, m, m)), dma((n, 2, m, m)),
            dma((n, 2, m, m)), dma((n, 2, m, m)),
            dma((n, 2, Y, X)), dma((n, 2, Y, X)),
            dma(()),
        ],
        compiler_params=pltpu.CompilerParams(
            collective_id=0, has_side_effects=True, vmem_limit_bytes=40 * 2**20
        ),
        name="gather",
    )(mine)


def tile_kernel(items, owner_ref, w_ref, out_ref, slot_of, code_of, used, turned, pick, mask, zeros, ring, sems, few):
    blocks, segs, groups, rows, width = w_ref.shape
    depth = segs * rows
    part_rows = width // ROW_PARTS
    slots = used.shape[0]
    buffers = ring.shape[0]
    me = lax.axis_index("chan")

    def store(source, slot):
        return pltpu.make_async_copy(source, out_ref.at[0, slot], sems.at[slot])

    def clear(k, _):
        used[k] = 0
        return 0

    lax.fori_loop(0, slots, clear, 0)

    def one_row(r, counts):
        n, m = counts
        for e in range(items):
            hit = owner_ref[r, e] == me
            real = hit & (r + e // ROW_PARTS < blocks)

            @pl.when(real)
            def _():
                used[n] = 1
                slot_of[m] = n
                code_of[m] = r * items + e

            n = n + hit.astype(jnp.int32)
            m = m + real.astype(jnp.int32)
        return n, m

    count = lax.fori_loop(0, blocks, one_row, (jnp.int32(0), jnp.int32(0)))[1]

    zeros[...] = jnp.zeros_like(zeros)

    def empty_start(k, _):
        @pl.when(used[k] == 0)
        def _():
            store(zeros, k).start()

        return 0

    lax.fori_loop(0, slots, empty_start, 0)

    def turn(b, _):
        for g in range(groups):
            w = w_ref[b, :, g].astype(jnp.float32).reshape(segs, 2, SUB, width)
            t = jnp.concatenate([-w[:, 1], w[:, 0]], axis=1)
            turned[b, :, g] = t.astype(jnp.bfloat16)
        return 0

    lax.fori_loop(0, blocks, turn, 0)
    row = lax.broadcasted_iota(jnp.int32, (part_rows * SUB, width), 0) // SUB
    col = lax.broadcasted_iota(jnp.int32, (part_rows * SUB, width), 1)
    few_row = lax.broadcasted_iota(jnp.int32, (part_rows, width), 0)
    for u in range(ROW_PARTS):
        pick[u] = jnp.where(row + u * part_rows == col, 1.0, 0.0).astype(jnp.bfloat16)
        few[u] = jnp.where(few_row + u * part_rows == col[:part_rows], 1.0, 0.0).astype(jnp.bfloat16)
    bin_row = lax.broadcasted_iota(jnp.int32, (SUB, depth), 0)
    bin_col = lax.broadcasted_iota(jnp.int32, (SUB, depth), 1) % SUB
    mask[...] = jnp.where(bin_row == bin_col, 1.0 / segs, 0.0)

    def one_tile(m, _):
        code = code_of[m]
        r = code // items
        e = code % items
        t = e // ROW_PARTS
        u = e % ROW_PARTS
        buf = m % buffers

        @pl.when(m >= buffers)
        def _():
            store(ring.at[buf], slot_of[lax.max(m - buffers, 0)]).wait()

        together = 2 if groups % 2 == 0 else 1
        for first in range(0, groups, together):
            results = []
            for g in range(first, first + together):
                w = w_ref[r, :, g].reshape(depth, width)
                if g % 2 == 0:
                    spread = nt_dot(pick[u], w).reshape(part_rows, SUB, depth)
                else:
                    spread = nt_dot(few[u], w)[:, None, :]
                left = (spread * mask[...][None]).reshape(part_rows * SUB, depth).astype(jnp.bfloat16)
                right = jnp.concatenate(
                    [w_ref[r + t, :, g].reshape(depth, width), turned[r + t, :, g].reshape(depth, width)],
                    axis=1,
                )
                results.append(dot(left, right).reshape(part_rows, SUB, 2 * width))
            both = jnp.concatenate(results, axis=1).astype(jnp.bfloat16)
            for i in range(part_rows):
                for a in range(2):
                    ring[buf, a, first * SUB : (first + together) * SUB, i * width : (i + 1) * width] = both[
                        i, :, a * width : (a + 1) * width
                    ]
        store(ring.at[buf], slot_of[m]).start()
        return 0

    lax.fori_loop(0, count, one_tile, 0)

    def last(m, _):
        store(ring.at[m % buffers], slot_of[m]).wait()
        return 0

    lax.fori_loop(lax.max(count - buffers, 0), count, last, 0)

    def empty_wait(k, _):
        @pl.when(used[k] == 0)
        def _():
            store(zeros, k).wait()

        return 0

    lax.fori_loop(0, slots, empty_wait, 0)


def tiles(gathered, tile_owner):
    blocks, segs, groups, rows, width = gathered.shape
    items = tile_owner.shape[1]
    slots = 2 * items
    depth = segs * rows
    part_rows = width // ROW_PARTS
    one = (2, groups * SUB, part_rows * width)
    buffers = 6
    return pl.pallas_call(
        partial(tile_kernel, items),
        in_specs=[
            pl.BlockSpec(memory_space=pltpu.SMEM),
            pl.BlockSpec(memory_space=pltpu.VMEM),
        ],
        out_specs=pl.BlockSpec(memory_space=pl.ANY),
        out_shape=jax.ShapeDtypeStruct((1, slots) + one, jnp.bfloat16),
        scratch_shapes=[
            pltpu.SMEM((slots,), jnp.int32),
            pltpu.SMEM((slots,), jnp.int32),
            pltpu.SMEM((slots,), jnp.int32),
            pltpu.VMEM(gathered.shape, jnp.bfloat16),
            pltpu.VMEM((ROW_PARTS, part_rows * SUB, width), jnp.bfloat16),
            pltpu.VMEM((SUB, depth), jnp.float32),
            pltpu.VMEM(one, jnp.bfloat16),
            pltpu.VMEM((buffers,) + one, jnp.bfloat16),
            pltpu.SemaphoreType.DMA((slots,)),
            pltpu.VMEM((ROW_PARTS, part_rows, width), jnp.bfloat16),
        ],
        compiler_params=pltpu.CompilerParams(vmem_limit_bytes=40 * 2**20),
        name="tiles",
    )(tile_owner, gathered)


def per_device(traces, live_first, live_end, tile_owner):
    white = whiten(traces, live_first, live_end, lax.axis_size("seg"))
    gathered = gather(white, lax.axis_size("chan"))
    return tiles(gathered, tile_owner)


def solution(mesh):
    placed = (P("seg", "chan", None), P("chan"), P("chan"), P())
    return jax.shard_map(
        per_device,
        mesh=mesh,
        in_specs=placed,
        out_specs=P("chan", None, None, "seg", None),
        check_vma=False,
    )
```

```python
from functools import partial
import math

import jax
import jax.numpy as jnp
import ml_dtypes
import numpy as np
from jax import lax
from jax.experimental import pallas as pl
from jax.experimental.pallas import tpu as pltpu
from jax.sharding import PartitionSpec as P

SAMPLES = 1792
BINS = 128
F_LOW = 20
SMOOTH = 64
TILES = 3
ROW_PARTS = 4
EPSILON = 1e-06
SUB = 8
MESH = pl.DeviceIdType.MESH


def wave_rows():
    t = np.arange(SAMPLES, dtype=np.int64)
    row = np.arange(2 * BINS)
    bin_of = row // (2 * SUB) * SUB + row % SUB
    part = row // SUB % 2
    phase = (t[None, :] * (F_LOW + bin_of)[:, None]) % SAMPLES
    angle = 2.0 * math.pi / SAMPLES * phase
    taper = 0.5 - 0.5 * np.cos(2.0 * math.pi / SAMPLES * (t + 0.5))
    wave = np.where(part[:, None] == 0, np.cos(angle), -np.sin(angle))
    return (taper[None, :] * wave).astype(np.float32).astype(ml_dtypes.bfloat16)


def nt_dot(a, b):
    return lax.dot_general(a, b, (((1,), (1,)), ((), ())), preferred_element_type=jnp.float32)


def dot(a, b):
    return jnp.dot(a, b, preferred_element_type=jnp.float32)


def whiten_kernel(first_ref, end_ref, traces_ref, wave_ref, out_ref):
    segs, width, samples = traces_ref.shape
    pieces, groups = out_ref.shape[0], out_ref.shape[2]
    cols = segs * width
    spec = nt_dot(wave_ref[...], traces_ref[...].reshape(cols, samples))
    spec = spec.reshape(BINS // SUB, 2, SUB, cols)
    power = (spec[:, 0] * spec[:, 0] + spec[:, 1] * spec[:, 1]).reshape(BINS, cols)
    to = lax.broadcasted_iota(jnp.int32, (BINS, BINS), 0)
    frm = lax.broadcasted_iota(jnp.int32, (BINS, BINS), 1)
    lowest = jnp.clip(to - SMOOTH // 2, 0, BINS - SMOOTH)
    inside = (frm >= lowest) & (frm < lowest + SMOOTH)
    window = jnp.where(inside, 1.0 / SMOOTH, 0.0).astype(jnp.bfloat16)
    high = power.astype(jnp.bfloat16)
    rest = power - high.astype(jnp.float32)
    mid = rest.astype(jnp.bfloat16)
    low = (rest - mid.astype(jnp.float32)).astype(jnp.bfloat16)
    smoothed = dot(window, high) + dot(window, mid) + dot(window, low)
    channel = lax.broadcasted_iota(jnp.int32, (BINS, cols), 1) % width
    live = (channel >= first_ref[0]) & (channel < end_ref[0])
    scaling = jnp.where(live, lax.rsqrt(smoothed + EPSILON), 0.0)
    white = spec * scaling.reshape(BINS // SUB, 1, SUB, cols)
    white = white.reshape(BINS // SUB, 2 * SUB, cols).astype(jnp.bfloat16)
    for s in range(segs):
        part = white[:, :, s * width : (s + 1) * width]
        out_ref[:, s] = part.reshape(pieces, groups, 2 * SUB, width)


def whiten(traces, live_first, live_end, pieces):
    segs, width, samples = traces.shape
    groups = BINS // SUB // pieces
    return pl.pallas_call(
        whiten_kernel,
        in_specs=[
            pl.BlockSpec(memory_space=pltpu.SMEM),
            pl.BlockSpec(memory_space=pltpu.SMEM),
            pl.BlockSpec(memory_space=pltpu.VMEM),
            pl.BlockSpec(memory_space=pltpu.VMEM),
        ],
        out_specs=pl.BlockSpec(memory_space=pltpu.VMEM),
        out_shape=jax.ShapeDtypeStruct((pieces, segs, groups, 2 * SUB, width), jnp.bfloat16),
        compiler_params=pltpu.CompilerParams(vmem_limit_bytes=40 * 2**20),
        name="whiten",
    )(live_first, live_end, traces, jnp.asarray(wave_rows()))


def gather_kernel(dims, mine_ref, out_ref, z_send, z_recv, x_send, x_recv, y_send, y_recv, c_send, c_recv, own_sem):
    X, Y, Z = dims
    segs = mine_ref.shape[1]
    half = segs // 2
    c = lax.axis_index("chan")
    z = lax.axis_index("seg")
    core = c % 2
    x = c // 2 % X
    y = c // 2 // X

    def chan(yy, xx, cc):
        return (yy * X + xx) * 2 + cc

    xs = [lax.rem(x + d, X) for d in range(X)]
    ys = [lax.rem(y + d, Y) for d in range(Y)]
    x_from = [lax.rem(x + X - d, X) for d in range(X)]
    y_from = [lax.rem(y + Y - d, Y) for d in range(Y)]
    zs = [lax.rem(z + d, Z) for d in range(Z)]
    z_from = [lax.rem(z + Z - d, Z) for d in range(Z)]
    sibling = chan(y, x, 1 - core)

    barrier = pltpu.get_barrier_semaphore()
    friends = [(c, zs[d]) for d in range(1, Z)]
    friends += [(chan(y, xs[d], core), z) for d in range(1, X)]
    friends += [(chan(ys[d], x, core), z) for d in range(1, Y)]
    friends += [(sibling, z)]
    for f in friends:
        pl.semaphore_signal(barrier, inc=1, device_id=f, device_id_type=MESH)
    pl.semaphore_wait(barrier, len(friends))

    started = []

    def block(owner, lo, count):
        return out_ref.at[owner, pl.ds(lo, count)]

    own = pltpu.make_async_copy(mine_ref.at[z], block(c, z * segs, segs), own_sem)
    own.start()
    for d in range(1, Z):
        copy = pltpu.make_async_remote_copy(
            mine_ref.at[zs[d]], block(c, z * segs, segs), z_send.at[d], z_recv.at[d],
            device_id=(c, zs[d]), device_id_type=MESH)
        copy.start()
        started.append(copy)

    def wait_z(d):
        if d == 0:
            own.wait()
        else:
            piece = block(c, z_from[d] * segs, segs)
            pltpu.make_async_remote_copy(
                piece, piece, z_send.at[d], z_recv.at[d], device_id=(c, z_from[d]), device_id_type=MESH
            ).wait_recv()

    if Z <= 4:
        order = sorted(range(Z), key=lambda d: min(d, Z - d))
        chunks = [((d,), z_from[d] * segs, half) for d in order]
    else:
        chunks = [(tuple(range(Z)), 0, Z * half)]

    def send(ref, send_sem, recv_sem, to):
        copy = pltpu.make_async_remote_copy(
            ref, ref, send_sem, recv_sem, device_id=(to, z), device_id_type=MESH)
        copy.start()
        started.append(copy)

    def wait_recv(ref, send_sem, recv_sem):
        pltpu.make_async_remote_copy(
            ref, ref, send_sem, recv_sem, device_id=(sibling, z), device_id_type=MESH
        ).wait_recv()

    def first_hops(k):
        waits, lo, count = chunks[k]
        for d in waits:
            wait_z(d)
        a, b = block(c, lo, count), block(c, lo + count, count)
        for d in range(1, X):
            send(a, x_send.at[k, 0, 0, d], x_recv.at[k, 0, 0, d], chan(y, xs[d], core))
        for d in range(1, Y):
            send(b, y_send.at[k, 1, 0, d], y_recv.at[k, 1, 0, d], chan(ys[d], x, core))
        for d in range(1, Y):
            send(a, y_send.at[k, 0, 0, d], y_recv.at[k, 0, 0, d], chan(ys[d], x, core))
        for d in range(1, X):
            send(b, x_send.at[k, 1, 0, d], x_recv.at[k, 1, 0, d], chan(y, xs[d], core))
        for h, ref in ((0, a), (1, b)):
            send(ref, c_send.at[k, h, 0, 0], c_recv.at[k, h, 0, 0], sibling)

    def second_hops(k):
        _, lo, count = chunks[k]
        for dx in range(1, X):
            a = block(chan(y, x_from[dx], core), lo, count)
            wait_recv(a, x_send.at[k, 0, 0, dx], x_recv.at[k, 0, 0, dx])
            for d in range(1, Y):
                send(a, y_send.at[k, 0, dx, d], y_recv.at[k, 0, dx, d], chan(ys[d], x, core))
            send(a, c_send.at[k, 0, 0, dx], c_recv.at[k, 0, 0, dx], sibling)
        for dy in range(1, Y):
            b = block(chan(y_from[dy], x, core), lo + count, count)
            wait_recv(b, y_send.at[k, 1, 0, dy], y_recv.at[k, 1, 0, dy])
            for d in range(1, X):
                send(b, x_send.at[k, 1, dy, d], x_recv.at[k, 1, dy, d], chan(y, xs[d], core))
            send(b, c_send.at[k, 1, dy, 0], c_recv.at[k, 1, dy, 0], sibling)

    def last_hops(k):
        _, lo, count = chunks[k]
        for dx in range(X):
            for dy in range(1, Y):
                a = block(chan(y_from[dy], x_from[dx], core), lo, count)
                wait_recv(a, y_send.at[k, 0, dx, dy], y_recv.at[k, 0, dx, dy])
                send(a, c_send.at[k, 0, dy, dx], c_recv.at[k, 0, dy, dx], sibling)
        for dy in range(Y):
            for dx in range(1, X):
                b = block(chan(y_from[dy], x_from[dx], core), lo + count, count)
                wait_recv(b, x_send.at[k, 1, dy, dx], x_recv.at[k, 1, dy, dx])
                send(b, c_send.at[k, 1, dy, dx], c_recv.at[k, 1, dy, dx], sibling)

    n = len(chunks)
    first_hops(0)
    second_hops(0)
    for k in range(1, n):
        first_hops(k)
    for k in range(1, n):
        second_hops(k)
    for k in range(n):
        last_hops(k)
    for k in range(n):
        _, lo, count = chunks[k]
        for h in range(2):
            for dy in range(Y):
                for dx in range(X):
                    ref = block(chan(y_from[dy], x_from[dx], 1 - core), lo + h * count, count)
                    wait_recv(ref, c_send.at[k, h, dy, dx], c_recv.at[k, h, dy, dx])
    for copy in started:
        copy.wait_send()


def gather(mine, chan_count):
    Z, segs, groups, rows, width = mine.shape
    X = math.isqrt(chan_count // 2)
    Y = chan_count // 2 // X
    n = Z if Z <= 4 else 1
    m = max(X, Y)
    dma = pltpu.SemaphoreType.DMA
    return pl.pallas_call(
        partial(gather_kernel, (X, Y, Z)),
        in_specs=[pl.BlockSpec(memory_space=pltpu.VMEM)],
        out_specs=pl.BlockSpec(memory_space=pltpu.VMEM),
        out_shape=jax.ShapeDtypeStruct((chan_count, Z * segs, groups, rows, width), mine.dtype),
        scratch_shapes=[
            dma((Z,)), dma((Z,)),
            dma((n, 2, m, m)), dma((n, 2, m, m)),
            dma((n, 2, m, m)), dma((n, 2, m, m)),
            dma((n, 2, Y, X)), dma((n, 2, Y, X)),
            dma(()),
        ],
        compiler_params=pltpu.CompilerParams(
            collective_id=0, has_side_effects=True, vmem_limit_bytes=40 * 2**20
        ),
        name="gather",
    )(mine)


def tile_kernel(items, owner_ref, w_ref, out_ref, slot_of, code_of, used, turned, pick, mask, zeros, ring, sems, few):
    blocks, segs, groups, rows, width = w_ref.shape
    depth = segs * rows
    part_rows = width // ROW_PARTS
    slots = used.shape[0]
    buffers = ring.shape[0]
    me = lax.axis_index("chan")

    def store(source, slot):
        return pltpu.make_async_copy(source, out_ref.at[0, slot], sems.at[slot])

    def clear(k, _):
        used[k] = 0
        return 0

    lax.fori_loop(0, slots, clear, 0)

    def one_row(r, counts):
        n, m = counts
        for e in range(items):
            hit = owner_ref[r, e] == me
            real = hit & (r + e // ROW_PARTS < blocks)

            @pl.when(real)
            def _():
                used[n] = 1
                slot_of[m] = n
                code_of[m] = r * items + e

            n = n + hit.astype(jnp.int32)
            m = m + real.astype(jnp.int32)
        return n, m

    count = lax.fori_loop(0, blocks, one_row, (jnp.int32(0), jnp.int32(0)))[1]

    zeros[...] = jnp.zeros_like(zeros)

    def empty_start(k, _):
        @pl.when(used[k] == 0)
        def _():
            store(zeros, k).start()

        return 0

    lax.fori_loop(0, slots, empty_start, 0)

    def turn(b, _):
        for g in range(groups):
            w = w_ref[b, :, g].astype(jnp.float32).reshape(segs, 2, SUB, width)
            t = jnp.concatenate([-w[:, 1], w[:, 0]], axis=1)
            turned[b, :, g] = t.astype(jnp.bfloat16)
        return 0

    lax.fori_loop(0, blocks, turn, 0)
    row = lax.broadcasted_iota(jnp.int32, (part_rows * SUB, width), 0) // SUB
    col = lax.broadcasted_iota(jnp.int32, (part_rows * SUB, width), 1)
    few_row = lax.broadcasted_iota(jnp.int32, (part_rows, width), 0)
    for u in range(ROW_PARTS):
        pick[u] = jnp.where(row + u * part_rows == col, 1.0, 0.0).astype(jnp.bfloat16)
        few[u] = jnp.where(few_row + u * part_rows == col[:part_rows], 1.0, 0.0).astype(jnp.bfloat16)
    bin_row = lax.broadcasted_iota(jnp.int32, (SUB, depth), 0)
    bin_col = lax.broadcasted_iota(jnp.int32, (SUB, depth), 1) % SUB
    mask[...] = jnp.where(bin_row == bin_col, 1.0 / segs, 0.0)

    def one_tile(m, _):
        code = code_of[m]
        r = code // items
        e = code % items
        t = e // ROW_PARTS
        u = e % ROW_PARTS
        buf = m % buffers

        @pl.when(m >= buffers)
        def _():
            store(ring.at[buf], slot_of[lax.max(m - buffers, 0)]).wait()

        together = 2 if groups % 2 == 0 else 1
        for first in range(0, groups, together):
            results = []
            for g in range(first, first + together):
                w = w_ref[r, :, g].reshape(depth, width)
                if g % 2 == 0:
                    spread = nt_dot(pick[u], w).reshape(part_rows, SUB, depth)
                else:
                    spread = nt_dot(few[u], w)[:, None, :]
                left = (spread * mask[...][None]).reshape(part_rows * SUB, depth).astype(jnp.bfloat16)
                right = jnp.concatenate(
                    [w_ref[r + t, :, g].reshape(depth, width), turned[r + t, :, g].reshape(depth, width)],
                    axis=1,
                )
                results.append(dot(left, right).reshape(part_rows, SUB, 2 * width))
            both = jnp.concatenate(results, axis=1).astype(jnp.bfloat16)
            for i in range(part_rows):
                for a in range(2):
                    ring[buf, a, first * SUB : (first + together) * SUB, i * width : (i + 1) * width] = both[
                        i, :, a * width : (a + 1) * width
                    ]
        store(ring.at[buf], slot_of[m]).start()
        return 0

    lax.fori_loop(0, count, one_tile, 0)

    def last(m, _):
        store(ring.at[m % buffers], slot_of[m]).wait()
        return 0

    lax.fori_loop(lax.max(count - buffers, 0), count, last, 0)

    def empty_wait(k, _):
        @pl.when(used[k] == 0)
        def _():
            store(zeros, k).wait()

        return 0

    lax.fori_loop(0, slots, empty_wait, 0)


def tiles(gathered, tile_owner):
    blocks, segs, groups, rows, width = gathered.shape
    items = tile_owner.shape[1]
    slots = 2 * items
    depth = segs * rows
    part_rows = width // ROW_PARTS
    one = (2, groups * SUB, part_rows * width)
    buffers = 6
    return pl.pallas_call(
        partial(tile_kernel, items),
        in_specs=[
            pl.BlockSpec(memory_space=pltpu.SMEM),
            pl.BlockSpec(memory_space=pltpu.VMEM),
        ],
        out_specs=pl.BlockSpec(memory_space=pl.ANY),
        out_shape=jax.ShapeDtypeStruct((1, slots) + one, jnp.bfloat16),
        scratch_shapes=[
            pltpu.SMEM((slots,), jnp.int32),
            pltpu.SMEM((slots,), jnp.int32),
            pltpu.SMEM((slots,), jnp.int32),
            pltpu.VMEM(gathered.shape, jnp.bfloat16),
            pltpu.VMEM((ROW_PARTS, part_rows * SUB, width), jnp.bfloat16),
            pltpu.VMEM((SUB, depth), jnp.float32),
            pltpu.VMEM(one, jnp.bfloat16),
            pltpu.VMEM((buffers,) + one, jnp.bfloat16),
            pltpu.SemaphoreType.DMA((slots,)),
            pltpu.VMEM((ROW_PARTS, part_rows, width), jnp.bfloat16),
        ],
        compiler_params=pltpu.CompilerParams(vmem_limit_bytes=40 * 2**20),
        name="tiles",
    )(tile_owner, gathered)


def per_device(traces, live_first, live_end, tile_owner):
    white = whiten(traces, live_first, live_end, lax.axis_size("seg"))
    gathered = gather(white, lax.axis_size("chan"))
    return tiles(gathered, tile_owner)


def solution(mesh):
    placed = (P("seg", "chan", None), P("chan"), P("chan"), P())
    return jax.shard_map(
        per_device,
        mesh=mesh,
        in_specs=placed,
        out_specs=P("chan", None, None, "seg", None),
        check_vma=False,
    )
```
